512 devices in a mesh: feat: 32 (over z, core), node: 16 (over x, y).
Axes of the slice: x: 4, y: 4, z: 16, core: 2. Of those that a mesh axis runs over, the one named last changes fastest.
Arguments:
- features: bfloat16 [16384, 1024], P('node', 'feat'), may hold values from -6 to 6
- target_feats: bfloat16 [16384, 1024], P('node', 'feat'), may hold values from -6 to 6
- tile_values: bfloat16 [512, 128, 128], P('node'), may hold values from 0 to 0.088378906
- tile_index: int32 [512, 2], P('node'), may hold values from 0 to 127, as said below
- tile_count: int32 [16], P('node'), may hold values from 8 to 32, as said below
- self_weight1: bfloat16 [1024, 256], P('feat'), may hold values from -0.1875 to 0.1875
- neigh_weight1: bfloat16 [1024, 256], P('feat'), may hold values from -0.1875 to 0.1875
- self_weight2: bfloat16 [256, 256], replicated, may hold values from -0.375 to 0.375
- neigh_weight2: bfloat16 [256, 256], replicated, may hold values from -0.375 to 0.375
- neighbors: int32 [4096, 10], P('node'), may hold values from 0 to 1023
- seed_index: int32 [4096], P('node'), may hold values from 0 to 1023, as said below
- cotangent: bfloat16 [4096, 256], P('node'), may hold values from -6 to 6
Outputs:
- output: bfloat16 [4096, 256], P('node')
- grad_w1: float32 [2, 1024, 256], P(None, 'feat')
- grad_w2: float32 [2, 256, 256], P(None, 'feat')
The draws below stay inside these ranges and needn't reach their ends.
Inputs may be any that keep to these rules, and one draw needn't show every extreme that they name: `tile_index`: column 0 names a block of 128 layer-one targets among all 16384; column 1 a block of 128 sources among the 1024 stored on the slot's own node index. A node index uses the first tile_count slots of its 32; some node index uses all of them. `seed_index`: the seeds of one node index are distinct targets of it.
All inputs are finite; a program needn't handle non-finite values.
Results may differ from the reference program's by a relative error of at most 0.0058.
Values may be sent and summed in bfloat16 or wider, within the bound.
No kernel may reach another device: no remote copies, remote signals or barrier semaphores. Data moves between devices by JAX's collectives and lax.ppermute only.
A program may use at most 64 MiB of HBM per device.

```python
import jax
import jax.numpy as jnp
from jax import lax

F = 1024
H = 256
BLK = 128
FAN = 10
SRC_DEV = 1024
TGT_DEV = 1024
SEED_DEV = 256
TILE_CAP = 32
TILES = 512
SOURCES = 16384
TARGETS = 16384
SEEDS = 4096
N_NODE = 16


def draw_tile_index(key, part):
    key = jax.random.fold_in(key, 11)
    first_key, second_key = jax.random.split(key)
    target_block = jax.random.randint(first_key, (TILES, 1), 0, TARGETS // BLK)
    source_block = jax.random.randint(second_key, (TILES, 1), 0, SRC_DEV // BLK)
    return jnp.concatenate([target_block, source_block], axis=1).astype(jnp.int32)


def draw_tile_count(key, part):
    key = jax.random.fold_in(key, 12)
    first_key, second_key = jax.random.split(key)
    counts = jax.random.randint(first_key, (N_NODE,), TILE_CAP // 4, TILE_CAP // 2 + 1)
    busiest = jax.random.randint(second_key, (), 0, N_NODE)
    full_slots = jnp.full((N_NODE,), TILE_CAP, jnp.int32)
    return jnp.where(jnp.arange(N_NODE) == busiest, full_slots, counts).astype(jnp.int32)


def draw_seed_index(key, part):
    key = jax.random.fold_in(key, 13)
    group_keys = jax.random.split(key, N_NODE)
    orders = jax.vmap(lambda group_key: jax.random.permutation(group_key, TGT_DEV))(group_keys)
    return orders[:, :SEED_DEV].reshape(-1).astype(jnp.int32)


def place_ends(result, key, low, top_value):
    dims = result.shape
    spot = [jax.random.randint(jax.random.fold_in(key, axis), (), 0, dims[axis]) for axis in range(len(dims))]
    result = result.at[tuple(spot)].set(low)
    longest = dims.index(max(dims))
    spot[longest] = (spot[longest] + 1) % dims[longest]
    return result.at[tuple(spot)].set(top_value)


def shard_levels(key, extent, cuts, least, largest):
    def one(position, parts):
        heights = jax.random.uniform(jax.random.fold_in(jax.random.fold_in(key, 6), position), (parts,), jnp.float32, least / len(cuts), largest / len(cuts))
        return jnp.repeat(jnp.exp(heights), extent[position] // parts).reshape((-1,) + (1,) * (len(extent) - position - 1))

    level = one(*cuts[0])
    for cut in cuts[1:]:
        level = level * one(*cut)
    return level


def scatter_about(stream_key, extent, deviation, bound, pieces=(), kind=jnp.bfloat16):
    drawn = deviation * jax.random.normal(stream_key, extent, jnp.float32)
    if pieces:
        drawn = drawn * shard_levels(stream_key, extent, pieces, -0.22, 0.18)
    return jnp.clip(drawn, -bound, bound).astype(kind)


def setup_inputs(seed: int = 0) -> dict:
    streams_of = jax.random.split(jax.random.key(seed), 13)
    features = scatter_about(streams_of[0], (SOURCES, F), 1.0, 6.0, ((0, 16), (1, 32)))
    target_feats = scatter_about(streams_of[1], (TARGETS, F), 1.0, 6.0, ((0, 16), (1, 32)))
    tile_values = jnp.clip(0.088378906 * jax.random.uniform(streams_of[2], (TILES, BLK, BLK), jnp.float32) ** shard_levels(streams_of[2], (TILES, BLK, BLK), ((0, 16),), -0.2, 0.2), 0.0, 0.088378906).astype(jnp.bfloat16)
    tile_index = draw_tile_index(jax.random.fold_in(streams_of[12], 71), 0)
    tile_count = draw_tile_count(jax.random.fold_in(streams_of[12], 71), 0)
    self_weight1 = scatter_about(streams_of[5], (F, H), F ** -0.5, 0.1875, ((0, 32),))
    neigh_weight1 = scatter_about(streams_of[6], (F, H), F ** -0.5, 0.1875, ((0, 32),))
    self_weight2 = scatter_about(streams_of[7], (H, H), H ** -0.5, 0.375)
    neigh_weight2 = scatter_about(streams_of[8], (H, H), H ** -0.5, 0.375)
    neighbors = place_ends(jax.random.randint(streams_of[9], (SEEDS, FAN), 0, TGT_DEV), jax.random.fold_in(streams_of[9], 1), 0, TGT_DEV - 1).astype(jnp.int32)
    seed_index = draw_seed_index(jax.random.fold_in(streams_of[12], 71), 0)
    cotangent = scatter_about(streams_of[11], (SEEDS, H), 1.0, 6.0, ((0, 16),))
    return {"features": features, "target_feats": target_feats, "tile_values": tile_values, "tile_index": tile_index, "tile_count": tile_count, "self_weight1": self_weight1, "neigh_weight1": neigh_weight1, "self_weight2": self_weight2, "neigh_weight2": neigh_weight2, "neighbors": neighbors, "seed_index": seed_index, "cotangent": cotangent}


def silu_slope(values):
    sigmoid = jax.nn.sigmoid(values)
    return sigmoid * (1.0 + values * (1.0 - sigmoid))


def reference(features, target_feats, tile_values, tile_index, tile_count, self_weight1, neigh_weight1, self_weight2, neigh_weight2, neighbors, seed_index, cotangent):
    def add_tile(running, element):
        tile_block, tile_pairs, slot_number = element
        owner_index = slot_number // TILE_CAP
        in_use = ((slot_number % TILE_CAP) < tile_count[owner_index]).astype(jnp.float32)
        first_row = (owner_index * SRC_DEV + tile_pairs[1] * BLK).astype(jnp.int32)
        source_rows = lax.dynamic_slice_in_dim(features, first_row, BLK, 0)
        product = jnp.dot(tile_block, source_rows, preferred_element_type=jnp.float32) * in_use
        return running.at[tile_pairs[0]].add(product), None

    start_sum = jnp.zeros((TARGETS // BLK, BLK, F), jnp.float32)
    slots = jnp.arange(TILES, dtype=jnp.int32)
    aggregate, _ = lax.scan(add_tile, start_sum, (tile_values, tile_index, slots))
    agg_half = aggregate.reshape(TARGETS, F).astype(jnp.bfloat16)
    pre_one = jnp.dot(target_feats, self_weight1, preferred_element_type=jnp.float32) + jnp.dot(agg_half, neigh_weight1, preferred_element_type=jnp.float32)
    hidden = jax.nn.silu(pre_one).astype(jnp.bfloat16)
    offsets = ((jnp.arange(SEEDS, dtype=jnp.int32) // SEED_DEV) * TGT_DEV).astype(jnp.int32)
    nbr_global = neighbors + offsets[:, None]
    seed_global = seed_index + offsets
    own = hidden[seed_global]
    nbr_mean = (jnp.sum(hidden[nbr_global].astype(jnp.float32), axis=1) / FAN).astype(jnp.bfloat16)
    pre_two = jnp.dot(own, self_weight2, preferred_element_type=jnp.float32) + jnp.dot(nbr_mean, neigh_weight2, preferred_element_type=jnp.float32)
    output = jax.nn.silu(pre_two).astype(jnp.bfloat16)
    slope_two = (cotangent.astype(jnp.float32) * silu_slope(pre_two)).astype(jnp.bfloat16)
    grad_w2 = jnp.stack([jnp.dot(own.T, slope_two, preferred_element_type=jnp.float32), jnp.dot(nbr_mean.T, slope_two, preferred_element_type=jnp.float32)])
    back_mean = jnp.dot(slope_two, neigh_weight2.T, preferred_element_type=jnp.float32) / FAN
    back_self = jnp.dot(slope_two, self_weight2.T, preferred_element_type=jnp.float32)
    spread = jnp.broadcast_to(back_mean[:, None, :], (SEEDS, FAN, H)).reshape(SEEDS * FAN, H)
    back_hidden = jnp.zeros((TARGETS, H), jnp.float32).at[nbr_global.reshape(-1)].add(spread).at[seed_global].add(back_self)
    slope_one = (back_hidden * silu_slope(pre_one)).astype(jnp.bfloat16)
    grad_w1 = jnp.stack([jnp.dot(target_feats.T, slope_one, preferred_element_type=jnp.float32), jnp.dot(agg_half.T, slope_one, preferred_element_type=jnp.float32)])
    return output, grad_w1, grad_w2
```

```python
import jax
import jax.numpy as jnp
from jax import lax
from jax.experimental import pallas as pl
from jax.experimental.pallas import tpu as pltpu
from jax.sharding import Mesh
from jax.sharding import PartitionSpec as P

BF16 = jnp.bfloat16
F32 = jnp.float32
NODE = ("x", "y")
FEAT = ("zh", "zl", "c")
MIB = 1 << 20

VMEM = pl.BlockSpec(memory_space=pltpu.VMEM)
SMEM = pl.BlockSpec(memory_space=pltpu.SMEM)


def contract(left, right, left_dim, right_dim):
    return lax.dot_general(
        left, right, (((left_dim,), (right_dim,)), ((), ())), preferred_element_type=F32
    )


def aggregate_kernel(count_ref, index_ref, tiles_ref, feats_ref, out_ref, sources, total):
    slots, block, _ = tiles_ref.shape
    for position in range(sources.shape[0]):
        sources[position] = feats_ref[:, position * block : (position + 1) * block]
    total[...] = jnp.zeros_like(total)
    live_tiles = count_ref[0]
    for slot in range(slots):
        target = index_ref[0, slot]
        source = index_ref[1, slot]
        in_use = (slot < live_tiles).astype(F32)
        product = contract(sources[source], tiles_ref[slot], 1, 1)
        total[target] += product * in_use
    out_ref[...] = total[...].astype(BF16)


def partial_kernel(core_ref, parts_ref, targets_ref, self_ref, neigh_ref, agg_ref, keep_ref, send_ref, halves):
    columns = targets_ref.shape[0]
    block = parts_ref.shape[2]
    owned = parts_ref[0].astype(F32)
    for position in range(1, parts_ref.shape[0]):
        owned += parts_ref[position].astype(F32)
    owned = owned.astype(BF16)
    for position in range(owned.shape[0] // columns):
        agg_ref[:, position * block : (position + 1) * block] = owned[
            position * columns : (position + 1) * columns
        ]
    inputs = jnp.concatenate([targets_ref[...], agg_ref[...]], axis=0)
    weights = jnp.concatenate([self_ref[...], neigh_ref[...]], axis=0)
    partial_pre = contract(inputs, weights, 0, 0)
    half = halves.shape[1]
    halves[0] = partial_pre[:half]
    halves[1] = partial_pre[half:]
    core = core_ref[0]
    keep_ref[...] = halves[core]
    send_ref[...] = halves[1 - core].astype(BF16)


def step_kernel(
    feat_ref,
    pre_ref,
    neighbors_ref,
    seeds_ref,
    self_ref,
    neigh_ref,
    cotangent_ref,
    targets_ref,
    agg_ref,
    output_ref,
    grads_ref,
    picks,
    scratch,
):
    rows = pre_ref.shape[0]
    fanout, seeds = neighbors_ref.shape
    columns = targets_ref.shape[0]
    row_of = lax.broadcasted_iota(jnp.int32, (rows, seeds), 0)
    counts = jnp.zeros((rows, seeds), F32)
    for entry in range(fanout):
        counts += (row_of == neighbors_ref[entry : entry + 1, :]).astype(F32)
    picks[:, :seeds] = counts.astype(BF16)
    picks[:, seeds:] = (row_of == seeds_ref[...]).astype(F32).astype(BF16)

    pre_one = pre_ref[...].astype(F32)
    sigmoid = jax.nn.sigmoid(pre_one)
    hidden = (pre_one * sigmoid).astype(BF16)
    gathered = contract(picks[...], hidden, 0, 0)
    nbr_mean = (gathered[:seeds] / fanout).astype(BF16)
    own = gathered[seeds:].astype(BF16)
    pre_two = contract(own, self_ref[...], 1, 0) + contract(nbr_mean, neigh_ref[...], 1, 0)
    gate = jax.nn.sigmoid(pre_two)
    output_ref[...] = (pre_two * gate).astype(BF16)
    slope_two = (
        cotangent_ref[...].astype(F32) * (gate * (1.0 + pre_two * (1.0 - gate)))
    ).astype(BF16)

    scratch[0] = contract(own, slope_two, 0, 0)
    scratch[1] = contract(nbr_mean, slope_two, 0, 0)

    back = jnp.concatenate(
        [contract(slope_two, neigh_ref[...], 1, 1) / fanout, contract(slope_two, self_ref[...], 1, 1)],
        axis=0,
    )
    back_high = back.astype(BF16)
    back_low = (back - back_high.astype(F32)).astype(BF16)
    chosen = picks[...]
    back_hidden = contract(chosen, back_high, 1, 0) + contract(chosen, back_low, 1, 0)
    slope_one = (back_hidden * (sigmoid * (1.0 + pre_one * (1.0 - sigmoid)))).astype(BF16)
    inputs = jnp.concatenate([targets_ref[...], agg_ref[...]], axis=0)
    grad_one = contract(inputs, slope_one, 1, 0).astype(BF16)
    part_rows = (grads_ref.shape[1] - 2 * columns) // 2
    first = pl.multiple_of(feat_ref[0] * part_rows, part_rows)
    grad_two = jnp.concatenate(
        [scratch[0, pl.ds(first, part_rows), :], scratch[1, pl.ds(first, part_rows), :]], axis=0
    ).astype(BF16)
    every = jnp.concatenate([grad_one, grad_two], axis=0)
    for position in range(grads_ref.shape[0]):
        grads_ref[position] = every


def per_device(
    features,
    target_feats,
    tile_values,
    tile_index,
    tile_count,
    self_weight1,
    neigh_weight1,
    self_weight2,
    neigh_weight2,
    neighbors,
    seed_index,
    cotangent,
):
    src_rows, columns = features.shape
    tgt_rows = target_feats.shape[0]
    slots, block, _ = tile_values.shape
    hsize = self_weight2.shape[0]
    owners = lax.axis_size(NODE)
    feat_count = lax.axis_size(FEAT)
    part_rows = hsize // feat_count
    near, far = lax.axis_size("zl"), lax.axis_size("zh")
    all_blocks = tgt_rows * owners // block
    targets = target_feats.T
    core = lax.axis_index("c").reshape(1)
    feat = lax.axis_index(FEAT).reshape(1)

    with jax.named_scope("aggregate_tiles"):
        aggregate = pl.pallas_call(
            aggregate_kernel,
            out_shape=jax.ShapeDtypeStruct((all_blocks, columns, block), BF16),
            in_specs=[SMEM, SMEM, VMEM, VMEM],
            out_specs=VMEM,
            scratch_shapes=[
                pltpu.VMEM((src_rows // block, columns, block), BF16),
                pltpu.VMEM((all_blocks, columns, block), F32),
            ],
            compiler_params=pltpu.CompilerParams(vmem_limit_bytes=16 * MIB),
        )(tile_count, tile_index.T, tile_values, features.T)
    with jax.named_scope("aggregate_exchange"):
        parts = lax.all_to_all(
            aggregate.reshape(owners, tgt_rows // block * columns, block), NODE, 0, 0, tiled=True
        )
    half = tgt_rows // 2
    with jax.named_scope("partial_pre"):
        agg_half, keep, send = pl.pallas_call(
            partial_kernel,
            out_shape=[
                jax.ShapeDtypeStruct((columns, tgt_rows), BF16),
                jax.ShapeDtypeStruct((half, hsize), F32),
                jax.ShapeDtypeStruct((half, hsize), BF16),
            ],
            in_specs=[SMEM] + [VMEM] * 4,
            out_specs=[VMEM] * 3,
            scratch_shapes=[pltpu.VMEM((2, half, hsize), F32)],
            compiler_params=pltpu.CompilerParams(vmem_limit_bytes=16 * MIB),
        )(core, parts, targets, self_weight1, neigh_weight1)
    with jax.named_scope("pre_sum_cores"):
        pair = keep + lax.ppermute(send, "c", [(0, 1), (1, 0)]).astype(F32)
    with jax.named_scope("pre_sum_near"):
        rows = half // near
        blocks = lax.all_to_all(
            pair.astype(BF16).reshape(near, rows, hsize), "zl", 0, 0, tiled=True
        )
        quarter = jnp.sum(blocks.astype(F32), axis=0).astype(BF16)
    with jax.named_scope("pre_sum_far"):
        copies = lax.all_to_all(
            jnp.broadcast_to(quarter[None], (far, rows, hsize)), "zh", 0, 0, tiled=True
        )
        pre_rows = jnp.sum(copies.astype(F32), axis=0).astype(BF16)
    with jax.named_scope("pre_gather"):
        pre_one = lax.all_gather(pre_rows, ("c", "zl"), tiled=True)

    grad_rows = 2 * columns + 2 * part_rows
    with jax.named_scope("step"):
        output, grads = pl.pallas_call(
            step_kernel,
            out_shape=[
                jax.ShapeDtypeStruct(cotangent.shape, BF16),
                jax.ShapeDtypeStruct((owners, grad_rows, hsize), BF16),
            ],
            in_specs=[SMEM] + [VMEM] * 8,
            out_specs=[VMEM] * 2,
            scratch_shapes=[
                pltpu.VMEM((tgt_rows, 2 * neighbors.shape[0]), BF16),
                pltpu.VMEM((2, hsize, hsize), F32),
            ],
            compiler_params=pltpu.CompilerParams(vmem_limit_bytes=32 * MIB),
        )(
            feat,
            pre_one,
            neighbors.T,
            seed_index.reshape(1, -1),
            self_weight2,
            neigh_weight2,
            cotangent,
            targets,
            agg_half,
        )
    with jax.named_scope("grad_sum"):
        grads = lax.all_to_all(grads, NODE, 0, 0, tiled=True)
        grads = jnp.sum(grads.astype(F32), axis=0)
    grad_one = grads[: 2 * columns].reshape(2, columns, hsize)
    grad_two = grads[2 * columns :].reshape(2, part_rows, hsize)
    return (output, grad_one, grad_two)


def solution(mesh):
    fine = Mesh(mesh.devices.reshape(4, 4, 2, 4, 4), FEAT + NODE)
    placed = (
        P(NODE, FEAT),
        P(NODE, FEAT),
        P(NODE, None, None),
        P(NODE, None),
        P(NODE),
        P(FEAT, None),
        P(FEAT, None),
        P(),
        P(),
        P(NODE, None),
        P(NODE),
        P(NODE, None),
    )
    return jax.shard_map(
        per_device,
        mesh=fine,
        in_specs=placed,
        out_specs=(P(NODE, None), P(None, FEAT, None), P(None, FEAT, None)),
        check_vma=False,
    )
```

```python
import jax
import jax.numpy as jnp
from jax import lax
from jax.experimental import pallas as pl
from jax.experimental.pallas import tpu as pltpu
from jax.sharding import Mesh
from jax.sharding import PartitionSpec as P

BF16 = jnp.bfloat16
F32 = jnp.float32
NODE = ("x", "y")
DEPTH = ("z",)
FEAT = ("z", "c")
MIB = 1 << 20

VMEM = pl.BlockSpec(memory_space=pltpu.VMEM)
HBM = pl.BlockSpec(memory_space=pltpu.HBM)
SMEM = pl.BlockSpec(memory_space=pltpu.SMEM)


def contract(left, right, left_dim, right_dim):
    return lax.dot_general(
        left, right, (((left_dim,), (right_dim,)), ((), ())), preferred_element_type=F32
    )


def aggregate_kernel(
    count_ref, index_ref, tiles_ref, feats_ref, out_ref, tiles, feats, sources, total, tile_sem, feat_sem
):
    slots, block, _ = tiles.shape
    group = slots // tile_sem.shape[0]
    feat_copy = pltpu.make_async_copy(feats_ref, feats, feat_sem)
    feat_copy.start()
    tile_copies = []
    for position in range(tile_sem.shape[0]):
        span = pl.ds(position * group, group)
        copy = pltpu.make_async_copy(tiles_ref.at[span], tiles.at[span], tile_sem.at[position])
        copy.start()
        tile_copies.append(copy)
    total[...] = jnp.zeros_like(total)
    feat_copy.wait()
    for position in range(sources.shape[0]):
        sources[position] = feats[:, position * block : (position + 1) * block]
    live_tiles = count_ref[0]
    for slot in range(slots):
        if slot % group == 0:
            tile_copies[slot // group].wait()
        target = index_ref[0, slot]
        source = index_ref[1, slot]
        in_use = (slot < live_tiles).astype(F32)
        product = contract(sources[source], tiles[slot], 1, 1)
        total[target] += product * in_use
    out_ref[...] = total[...].astype(BF16)


def partial_kernel(core_ref, parts_ref, targets_ref, self_ref, neigh_ref, agg_ref, keep_ref, send_ref, halves):
    columns = targets_ref.shape[0]
    block = parts_ref.shape[2]
    owned = parts_ref[0].astype(F32)
    for position in range(1, parts_ref.shape[0]):
        owned += parts_ref[position].astype(F32)
    owned = owned.astype(BF16)
    for position in range(owned.shape[0] // columns):
        agg_ref[:, position * block : (position + 1) * block] = owned[
            position * columns : (position + 1) * columns
        ]
    inputs = jnp.concatenate([targets_ref[...], agg_ref[...]], axis=0)
    weights = jnp.concatenate([self_ref[...], neigh_ref[...]], axis=0)
    partial_pre = contract(inputs, weights, 0, 0)
    _, spans, span, _ = halves.shape
    for position in range(2 * spans):
        halves[position % 2, position // 2] = partial_pre[position * span : (position + 1) * span]
    core = core_ref[0]
    keep_ref[...] = halves[core]
    send_ref[...] = halves[1 - core]


def sum_kernel(parts_ref, out_ref):
    total = parts_ref[0].astype(F32)
    for position in range(1, parts_ref.shape[0]):
        total += parts_ref[position].astype(F32)
    out_ref[...] = total.astype(out_ref.dtype)


def grads_kernel(parts_ref, one_ref, two_ref):
    total = parts_ref[0].astype(F32)
    for position in range(1, parts_ref.shape[0]):
        total += parts_ref[position].astype(F32)
    columns, part_rows = one_ref.shape[1], two_ref.shape[1]
    one_ref[0] = total[:columns]
    one_ref[1] = total[columns : 2 * columns]
    two = total[2 * columns : 2 * columns + 2 * part_rows] + total[2 * columns + 2 * part_rows :]
    two_ref[0] = two[:part_rows]
    two_ref[1] = two[part_rows:]


def step_kernel(
    feat_ref,
    pre_ref,
    neighbors_ref,
    seeds_ref,
    self_ref,
    neigh_ref,
    cotangent_ref,
    targets_ref,
    agg_ref,
    output_ref,
    grads_ref,
    picks,
    scratch,
):
    rows = pre_ref.shape[0]
    fanout, seeds = neighbors_ref.shape
    columns = targets_ref.shape[0]
    row_of = lax.broadcasted_iota(jnp.int32, (rows, seeds), 0)
    counts = jnp.zeros((rows, seeds), F32)
    for entry in range(fanout):
        counts += (row_of == neighbors_ref[entry : entry + 1, :]).astype(F32)
    picks[:, :seeds] = counts.astype(BF16)
    picks[:, seeds:] = (row_of == seeds_ref[...]).astype(F32).astype(BF16)

    pre_one = pre_ref[...].astype(F32)
    sigmoid = jax.nn.sigmoid(pre_one)
    hidden = (pre_one * sigmoid).astype(BF16)
    gathered = contract(picks[...], hidden, 0, 0)
    nbr_mean = (gathered[:seeds] / fanout).astype(BF16)
    own = gathered[seeds:].astype(BF16)
    pre_two = contract(own, self_ref[...], 1, 0) + contract(nbr_mean, neigh_ref[...], 1, 0)
    gate = jax.nn.sigmoid(pre_two)
    output_ref[...] = (pre_two * gate).astype(BF16)
    slope_two = (
        cotangent_ref[...].astype(F32) * (gate * (1.0 + pre_two * (1.0 - gate)))
    ).astype(BF16)

    scratch[0] = contract(own, slope_two, 0, 0)
    scratch[1] = contract(nbr_mean, slope_two, 0, 0)

    back = jnp.concatenate(
        [contract(slope_two, neigh_ref[...], 1, 1) / fanout, contract(slope_two, self_ref[...], 1, 1)],
        axis=0,
    )
    back_high = back.astype(BF16)
    back_low = (back - back_high.astype(F32)).astype(BF16)
    chosen = picks[...]
    back_hidden = contract(chosen, back_high, 1, 0) + contract(chosen, back_low, 1, 0)
    slope_one = (back_hidden * (sigmoid * (1.0 + pre_one * (1.0 - sigmoid)))).astype(BF16)
    inputs = jnp.concatenate([targets_ref[...], agg_ref[...]], axis=0)
    grad_one = contract(inputs, slope_one, 1, 0).astype(BF16)
    part_rows = (grads_ref.shape[1] - 2 * columns) // 4
    first = pl.multiple_of(feat_ref[0] * part_rows, part_rows)
    grad_two = jnp.concatenate(
        [scratch[0, pl.ds(first, part_rows), :], scratch[1, pl.ds(first, part_rows), :]], axis=0
    )
    two_high = grad_two.astype(BF16)
    two_low = (grad_two - two_high.astype(F32)).astype(BF16)
    every = jnp.concatenate([grad_one, two_high, two_low], axis=0)
    for position in range(grads_ref.shape[0]):
        grads_ref[position] = every


def per_device(
    features,
    target_feats,
    tile_values,
    tile_index,
    tile_count,
    self_weight1,
    neigh_weight1,
    self_weight2,
    neigh_weight2,
    neighbors,
    seed_index,
    cotangent,
):
    src_rows, columns = features.shape
    tgt_rows = target_feats.shape[0]
    slots, block, _ = tile_values.shape
    hsize = self_weight2.shape[0]
    owners = lax.axis_size(NODE)
    feat_count = lax.axis_size(FEAT)
    part_rows = hsize // feat_count
    deep = lax.axis_size(DEPTH)
    span = tgt_rows // feat_count
    all_blocks = tgt_rows * owners // block
    targets = target_feats.T
    core = lax.axis_index("c").reshape(1)
    feat = lax.axis_index(FEAT).reshape(1)

    with jax.named_scope("aggregate_tiles"):
        aggregate = pl.pallas_call(
            aggregate_kernel,
            out_shape=pltpu.VMEM((all_blocks, columns, block), BF16),
            in_specs=[SMEM, SMEM, HBM, HBM],
            out_specs=VMEM,
            scratch_shapes=[
                pltpu.VMEM(tile_values.shape, BF16),
                pltpu.VMEM((columns, src_rows), BF16),
                pltpu.VMEM((src_rows // block, columns, block), BF16),
                pltpu.VMEM((all_blocks, columns, block), F32),
                pltpu.SemaphoreType.DMA((4,)),
                pltpu.SemaphoreType.DMA,
            ],
            compiler_params=pltpu.CompilerParams(vmem_limit_bytes=16 * MIB),
        )(tile_count, tile_index.T, tile_values, features.T)
    with jax.named_scope("aggregate_exchange"):
        parts = lax.all_to_all(
            aggregate.reshape(owners, tgt_rows // block * columns, block), NODE, 0, 0, tiled=True
        )
    with jax.named_scope("partial_pre"):
        agg_half, keep, send = pl.pallas_call(
            partial_kernel,
            out_shape=[
                jax.ShapeDtypeStruct((columns, tgt_rows), BF16),
                jax.ShapeDtypeStruct((deep, span, hsize), F32),
                jax.ShapeDtypeStruct((deep, span, hsize), F32),
            ],
            in_specs=[SMEM] + [VMEM] * 4,
            out_specs=[VMEM] * 3,
            scratch_shapes=[pltpu.VMEM((2, deep, span, hsize), F32)],
            compiler_params=pltpu.CompilerParams(vmem_limit_bytes=16 * MIB),
        )(core, parts, targets, self_weight1, neigh_weight1)
    with jax.named_scope("pre_sum_cores"):
        pair = (keep + lax.ppermute(send, "c", [(0, 1), (1, 0)])).astype(BF16)
    with jax.named_scope("pre_sum_depth"):
        pieces = lax.all_to_all(pair, DEPTH, 0, 0, tiled=True)
        pre_rows = pl.pallas_call(
            sum_kernel,
            out_shape=jax.ShapeDtypeStruct((span, hsize), BF16),
            in_specs=[VMEM],
            out_specs=VMEM,
        )(pieces)
    with jax.named_scope("pre_gather"):
        pre_one = lax.all_gather(pre_rows, FEAT, tiled=True)

    grad_rows = 2 * columns + 4 * part_rows
    with jax.named_scope("step"):
        output, grads = pl.pallas_call(
            step_kernel,
            out_shape=[
                jax.ShapeDtypeStruct(cotangent.shape, BF16),
                jax.ShapeDtypeStruct((owners, grad_rows, hsize), BF16),
            ],
            in_specs=[SMEM] + [VMEM] * 8,
            out_specs=[VMEM] * 2,
            scratch_shapes=[
                pltpu.VMEM((tgt_rows, 2 * neighbors.shape[0]), BF16),
                pltpu.VMEM((2, hsize, hsize), F32),
            ],
            compiler_params=pltpu.CompilerParams(vmem_limit_bytes=32 * MIB),
        )(
            feat,
            pre_one,
            neighbors.T,
            seed_index.reshape(1, -1),
            self_weight2,
            neigh_weight2,
            cotangent,
            targets,
            agg_half,
        )
    with jax.named_scope("grad_sum"):
        grads = lax.all_to_all(grads, NODE, 0, 0, tiled=True)
        grad_one, grad_two = pl.pallas_call(
            grads_kernel,
            out_shape=[
                jax.ShapeDtypeStruct((2, columns, hsize), F32),
                jax.ShapeDtypeStruct((2, part_rows, hsize), F32),
            ],
            in_specs=[VMEM],
            out_specs=[VMEM] * 2,
        )(grads)
    return (output, grad_one, grad_two)


def solution(mesh):
    fine = Mesh(mesh.devices.reshape(16, 2, 4, 4), FEAT + NODE)
    placed = (
        P(NODE, FEAT),
        P(NODE, FEAT),
        P(NODE, None, None),
        P(NODE, None),
        P(NODE),
        P(FEAT, None),
        P(FEAT, None),
        P(),
        P(),
        P(NODE, None),
        P(NODE),
        P(NODE, None),
    )
    return jax.shard_map(
        per_device,
        mesh=fine,
        in_specs=placed,
        out_specs=(P(NODE, None), P(None, FEAT, None), P(None, FEAT, None)),
        check_vma=False,
    )
```

```python
import jax
import jax.numpy as jnp
from jax import lax
from jax.experimental import pallas as pl
from jax.experimental.pallas import tpu as pltpu
from jax.sharding import Mesh
from jax.sharding import PartitionSpec as P

BF16 = jnp.bfloat16
F32 = jnp.float32
NODE = ("x", "y")
FEAT = ("zh", "zl", "c")
FAN = 10
MIB = 1 << 20

VMEM = pl.BlockSpec(memory_space=pltpu.VMEM)
HBM = pl.BlockSpec(memory_space=pltpu.HBM)
SMEM = pl.BlockSpec(memory_space=pltpu.SMEM)


def contract(left, right, left_dim, right_dim):
    return lax.dot_general(
        left, right, (((left_dim,), (right_dim,)), ((), ())), preferred_element_type=F32
    )


def aggregate_kernel(
    count_ref, index_ref, tiles_ref, feats_ref, out_ref, tiles, feats, sources, total, tile_sem, feat_sem
):
    slots, block, _ = tiles.shape
    group = slots // tile_sem.shape[0]
    feat_copy = pltpu.make_async_copy(feats_ref, feats, feat_sem)
    feat_copy.start()
    tile_copies = []
    for position in range(tile_sem.shape[0]):
        span = pl.ds(position * group, group)
        copy = pltpu.make_async_copy(tiles_ref.at[span], tiles.at[span], tile_sem.at[position])
        copy.start()
        tile_copies.append(copy)
    total[...] = jnp.zeros_like(total)
    feat_copy.wait()
    for position in range(sources.shape[0]):
        sources[position] = feats[:, position * block : (position + 1) * block]
    live_tiles = count_ref[0]
    for slot in range(slots):
        if slot % group == 0:
            tile_copies[slot // group].wait()
        target = index_ref[0, slot]
        source = index_ref[1, slot]
        in_use = (slot < live_tiles).astype(F32)
        product = contract(sources[source], tiles[slot], 1, 1)
        total[target] += product * in_use
    out_ref[...] = total[...].astype(BF16)


def partial_kernel(core_ref, parts_ref, targets_ref, self_ref, neigh_ref, agg_ref, keep_ref, send_ref, halves):
    columns = targets_ref.shape[0]
    block = parts_ref.shape[2]
    owned = parts_ref[0].astype(F32)
    for position in range(1, parts_ref.shape[0]):
        owned += parts_ref[position].astype(F32)
    owned = owned.astype(BF16)
    for position in range(owned.shape[0] // columns):
        agg_ref[:, position * block : (position + 1) * block] = owned[
            position * columns : (position + 1) * columns
        ]
    inputs = jnp.concatenate([targets_ref[...], agg_ref[...]], axis=0)
    weights = jnp.concatenate([self_ref[...], neigh_ref[...]], axis=0)
    partial_pre = contract(inputs, weights, 0, 0)
    _, spans, span, _ = halves.shape
    for position in range(2 * spans):
        halves[position % 2, position // 2] = partial_pre[position * span : (position + 1) * span]
    core = core_ref[0]
    keep_ref[...] = halves[core]
    send_ref[...] = halves[1 - core]


def sum_kernel(parts_ref, out_ref):
    total = parts_ref[0].astype(F32)
    for position in range(1, parts_ref.shape[0]):
        total += parts_ref[position].astype(F32)
    for position in range(out_ref.shape[0]):
        out_ref[position] = total.astype(out_ref.dtype)


def grads_kernel(parts_ref, one_ref, two_ref):
    total = parts_ref[0].astype(F32)
    for position in range(1, parts_ref.shape[0]):
        total += parts_ref[position].astype(F32)
    columns, part_rows = one_ref.shape[1], two_ref.shape[1]
    one_ref[0] = total[:columns]
    one_ref[1] = total[columns : 2 * columns]
    two = total[2 * columns : 2 * columns + 2 * part_rows] + total[2 * columns + 2 * part_rows :]
    two_ref[0] = two[:part_rows]
    two_ref[1] = two[part_rows:]


def picks_kernel(neighbors_ref, seeds_ref, picks_ref):
    fanout, seeds = neighbors_ref.shape
    rows = picks_ref.shape[0]
    row_of = lax.broadcasted_iota(jnp.int32, (rows, seeds), 0)
    counts = jnp.zeros((rows, seeds), F32)
    for entry in range(fanout):
        counts += (row_of == neighbors_ref[entry : entry + 1, :]).astype(F32)
    picks_ref[:, :seeds] = counts.astype(BF16)
    picks_ref[:, seeds:] = (row_of == seeds_ref[...]).astype(F32).astype(BF16)


def step_kernel(
    feat_ref,
    pre_ref,
    picks_ref,
    self_ref,
    neigh_ref,
    cotangent_ref,
    targets_ref,
    agg_ref,
    output_ref,
    grads_ref,
    scratch,
):
    seeds = cotangent_ref.shape[0]
    columns = targets_ref.shape[0]
    pre_one = pre_ref[...].astype(F32)
    sigmoid = jax.nn.sigmoid(pre_one)
    hidden = (pre_one * sigmoid).astype(BF16)
    gathered = contract(picks_ref[...], hidden, 0, 0)
    nbr_mean = (gathered[:seeds] / FAN).astype(BF16)
    own = gathered[seeds:].astype(BF16)
    pre_two = contract(own, self_ref[...], 1, 0) + contract(nbr_mean, neigh_ref[...], 1, 0)
    gate = jax.nn.sigmoid(pre_two)
    output_ref[...] = (pre_two * gate).astype(BF16)
    slope_two = (
        cotangent_ref[...].astype(F32) * (gate * (1.0 + pre_two * (1.0 - gate)))
    ).astype(BF16)

    scratch[0] = contract(own, slope_two, 0, 0)
    scratch[1] = contract(nbr_mean, slope_two, 0, 0)

    back = jnp.concatenate(
        [contract(slope_two, neigh_ref[...], 1, 1) / FAN, contract(slope_two, self_ref[...], 1, 1)],
        axis=0,
    )
    back_high = back.astype(BF16)
    back_low = (back - back_high.astype(F32)).astype(BF16)
    chosen = picks_ref[...]
    back_hidden = contract(chosen, back_high, 1, 0) + contract(chosen, back_low, 1, 0)
    slope_one = (back_hidden * (sigmoid * (1.0 + pre_one * (1.0 - sigmoid)))).astype(BF16)
    inputs = jnp.concatenate([targets_ref[...], agg_ref[...]], axis=0)
    grad_one = contract(inputs, slope_one, 1, 0).astype(BF16)
    part_rows = (grads_ref.shape[1] - 2 * columns) // 4
    first = pl.multiple_of(feat_ref[0] * part_rows, part_rows)
    grad_two = jnp.concatenate(
        [scratch[0, pl.ds(first, part_rows), :], scratch[1, pl.ds(first, part_rows), :]], axis=0
    )
    two_high = grad_two.astype(BF16)
    two_low = (grad_two - two_high.astype(F32)).astype(BF16)
    every = jnp.concatenate([grad_one, two_high, two_low], axis=0)
    for position in range(grads_ref.shape[0]):
        grads_ref[position] = every


def sum_pieces(pieces, copies):
    return pl.pallas_call(
        sum_kernel,
        out_shape=jax.ShapeDtypeStruct((copies,) + pieces.shape[1:], BF16),
        in_specs=[VMEM],
        out_specs=VMEM,
        compiler_params=pltpu.CompilerParams(vmem_limit_bytes=8 * MIB),
    )(pieces)


def per_device(
    features,
    target_feats,
    tile_values,
    tile_index,
    tile_count,
    self_weight1,
    neigh_weight1,
    self_weight2,
    neigh_weight2,
    neighbors,
    seed_index,
    cotangent,
):
    src_rows, columns = features.shape
    tgt_rows = target_feats.shape[0]
    slots, block, _ = tile_values.shape
    hsize = self_weight2.shape[0]
    seed_count = seed_index.shape[0]
    owners = lax.axis_size(NODE)
    feat_count = lax.axis_size(FEAT)
    part_rows = hsize // feat_count
    near, far = lax.axis_size("zl"), lax.axis_size("zh")
    span = tgt_rows // near // 2
    all_blocks = tgt_rows * owners // block
    targets = target_feats.T
    core = lax.axis_index("c").reshape(1)
    feat = lax.axis_index(FEAT).reshape(1)

    with jax.named_scope("aggregate_tiles"):
        aggregate = pl.pallas_call(
            aggregate_kernel,
            out_shape=pltpu.VMEM((all_blocks, columns, block), BF16),
            in_specs=[SMEM, SMEM, HBM, HBM],
            out_specs=VMEM,
            scratch_shapes=[
                pltpu.VMEM(tile_values.shape, BF16),
                pltpu.VMEM((columns, src_rows), BF16),
                pltpu.VMEM((src_rows // block, columns, block), BF16),
                pltpu.VMEM((all_blocks, columns, block), F32),
                pltpu.SemaphoreType.DMA((4,)),
                pltpu.SemaphoreType.DMA,
            ],
            compiler_params=pltpu.CompilerParams(vmem_limit_bytes=56 * MIB),
        )(tile_count, tile_index.T, tile_values, features.T)
    with jax.named_scope("aggregate_exchange"):
        parts = lax.all_to_all(
            aggregate.reshape(owners, tgt_rows // block * columns, block), NODE, 0, 0, tiled=True
        )
    with jax.named_scope("partial_pre"):
        agg_half, keep, send = pl.pallas_call(
            partial_kernel,
            out_shape=[
                jax.ShapeDtypeStruct((columns, tgt_rows), BF16),
                jax.ShapeDtypeStruct((near, span, hsize), F32),
                jax.ShapeDtypeStruct((near, span, hsize), F32),
            ],
            in_specs=[SMEM] + [VMEM] * 4,
            out_specs=[VMEM] * 3,
            scratch_shapes=[pltpu.VMEM((2, near, span, hsize), F32)],
            compiler_params=pltpu.CompilerParams(vmem_limit_bytes=16 * MIB),
        )(core, parts, targets, self_weight1, neigh_weight1)
    with jax.named_scope("pre_sum_cores"):
        pair = (keep + lax.ppermute(send, "c", [(0, 1), (1, 0)])).astype(BF16)
    with jax.named_scope("pre_sum_near"):
        pieces = lax.all_to_all(pair, "zl", 0, 0, tiled=True)
        copies = sum_pieces(pieces, far)
    with jax.named_scope("pre_sum_far"):
        copies = lax.all_to_all(copies, "zh", 0, 0, tiled=True)
        pre_rows = sum_pieces(copies, 1)[0]
    with jax.named_scope("pre_gather"):
        pre_one = lax.all_gather(pre_rows, ("zl", "c"), tiled=True)
    with jax.named_scope("picks"):
        picks = pl.pallas_call(
            picks_kernel,
            out_shape=jax.ShapeDtypeStruct((tgt_rows, 2 * seed_count), BF16),
            in_specs=[VMEM] * 2,
            out_specs=VMEM,
            cost_estimate=pl.CostEstimate(
                flops=20 * tgt_rows * seed_count, bytes_accessed=4 * tgt_rows * seed_count, transcendentals=0
            ),
            compiler_params=pltpu.CompilerParams(vmem_limit_bytes=16 * MIB),
        )(neighbors.T, seed_index.reshape(1, -1))

    grad_rows = 2 * columns + 4 * part_rows
    with jax.named_scope("step"):
        output, grads = pl.pallas_call(
            step_kernel,
            out_shape=[
                jax.ShapeDtypeStruct(cotangent.shape, BF16),
                jax.ShapeDtypeStruct((owners, grad_rows, hsize), BF16),
            ],
            in_specs=[SMEM] + [VMEM] * 7,
            out_specs=[VMEM] * 2,
            scratch_shapes=[pltpu.VMEM((2, hsize, hsize), F32)],
            compiler_params=pltpu.CompilerParams(vmem_limit_bytes=24 * MIB),
        )(
            feat,
            pre_one,
            picks,
            self_weight2,
            neigh_weight2,
            cotangent,
            targets,
            agg_half,
        )
    with jax.named_scope("grad_sum"):
        grads = lax.all_to_all(grads, NODE, 0, 0, tiled=True)
        grad_one, grad_two = pl.pallas_call(
            grads_kernel,
            out_shape=[
                jax.ShapeDtypeStruct((2, columns, hsize), F32),
                jax.ShapeDtypeStruct((2, part_rows, hsize), F32),
            ],
            in_specs=[VMEM],
            out_specs=[VMEM] * 2,
            compiler_params=pltpu.CompilerParams(vmem_limit_bytes=8 * MIB),
        )(grads)
    return (output, grad_one, grad_two)


def solution(mesh):
    fine = Mesh(mesh.devices.reshape(4, 4, 2, 4, 4), FEAT + NODE)
    placed = (
        P(NODE, FEAT),
        P(NODE, FEAT),
        P(NODE, None, None),
        P(NODE, None),
        P(NODE),
        P(FEAT, None),
        P(FEAT, None),
        P(),
        P(),
        P(NODE, None),
        P(NODE),
        P(NODE, None),
    )
    return jax.shard_map(
        per_device,
        mesh=fine,
        in_specs=placed,
        out_specs=(P(NODE, None), P(None, FEAT, None), P(None, FEAT, None)),
        check_vma=False,
    )
```

```python
import jax
import jax.numpy as jnp
from jax import lax
from jax.experimental import pallas as pl
from jax.experimental.pallas import tpu as pltpu
from jax.sharding import Mesh
from jax.sharding import PartitionSpec as P

BF16 = jnp.bfloat16
F32 = jnp.float32
NODE = ("x", "y")
FEAT = ("zh", "zl", "c")
FAN = 10
MIB = 1 << 20

VMEM = pl.BlockSpec(memory_space=pltpu.VMEM)
HBM = pl.BlockSpec(memory_space=pltpu.HBM)
ANY = pl.BlockSpec(memory_space=pl.ANY)
SMEM = pl.BlockSpec(memory_space=pltpu.SMEM)


def contract(left, right, left_dim, right_dim):
    return lax.dot_general(
        left, right, (((left_dim,), (right_dim,)), ((), ())), preferred_element_type=F32
    )


def aggregate_kernel(
    count_ref, index_ref, tiles_ref, feats_ref, out_ref, tiles, feats, sources, products, total, tile_sem, feat_sem
):
    slots, block, _ = tiles.shape
    group = slots // tile_sem.shape[0]
    feat_copy = pltpu.make_async_copy(feats_ref, feats, feat_sem)
    feat_copy.start()
    tile_copies = []
    for position in range(tile_sem.shape[0]):
        span = pl.ds(position * group, group)
        copy = pltpu.make_async_copy(tiles_ref.at[span], tiles.at[span], tile_sem.at[position])
        copy.start()
        tile_copies.append(copy)
    total[...] = jnp.zeros_like(total)
    feat_copy.wait()
    for position in range(sources.shape[0]):
        sources[position] = feats[:, position * block : (position + 1) * block]
    live_tiles = count_ref[0]
    for slot in range(slots):
        if slot % group == 0:
            tile_copies[slot // group].wait()
        in_use = (slot < live_tiles).astype(F32)
        products[slot] = contract(sources[index_ref[1, slot]], tiles[slot], 1, 1) * in_use
    for slot in range(slots):
        target = index_ref[0, slot]
        total[target] += products[slot]
    out_ref[...] = total[...].astype(BF16)


def split_blocks(core, halves, mine_ref, other_ref):
    block = halves.shape[3]
    for position in range(halves.shape[0]):
        span = slice(position * block, (position + 1) * block)
        mine_ref[:, span] = halves[position, core]
        other_ref[:, span] = halves[position, 1 - core]


def pack_kernel(core_ref, targets_ref, self_ref, neigh_ref, mine_ref, pack_ref, halves):
    columns = targets_ref.shape[0]
    near, _, _, block = halves.shape
    for position in range(2 * near):
        halves[position // 2, position % 2] = targets_ref[:, position * block : (position + 1) * block]
    split_blocks(core_ref[0], halves, mine_ref, pack_ref.at[:columns])
    hsize = self_ref.shape[1]
    pack_ref[columns:, :hsize] = self_ref[...]
    pack_ref[columns:, hsize:] = neigh_ref[...]


def owned_kernel(core_ref, parts_ref, mine_ref, other_ref, halves):
    near, _, columns, _ = halves.shape
    for position in range(2 * near):
        span = slice(position * columns, (position + 1) * columns)
        block = parts_ref[0, span].astype(F32)
        for source in range(1, parts_ref.shape[0]):
            block += parts_ref[source, span].astype(F32)
        halves[position // 2, position % 2] = block.astype(BF16)
    split_blocks(core_ref[0], halves, mine_ref, other_ref)


def partial_kernel(targets_ref, pack_ref, mine_ref, arrived_ref, self_ref, neigh_ref, out_ref):
    columns, hsize = self_ref.shape
    inputs = jnp.concatenate(
        [targets_ref[...], pack_ref[:columns], mine_ref[...], arrived_ref[...]], axis=0
    )
    weights = jnp.concatenate(
        [self_ref[...], pack_ref[columns:, :hsize], neigh_ref[...], pack_ref[columns:, hsize:]], axis=0
    )
    out_ref[...] = contract(inputs, weights, 0, 0).reshape(out_ref.shape).astype(BF16)


def near_kernel(parts_ref, out_ref):
    total = parts_ref[0].astype(F32)
    for position in range(1, parts_ref.shape[0]):
        total += parts_ref[position].astype(F32)
    out_ref[...] = total.astype(BF16)


def far_kernel(far_ref, own_ref, two_ref, one_ref, three_ref, picks_ref, out_ref, slots):
    far = far_ref[0]
    slots[far] = own_ref[...].astype(F32)
    for step, ref in ((2, two_ref), (1, one_ref), (3, three_ref)):
        slots[lax.rem(far + slots.shape[0] - step, slots.shape[0])] = ref[...].astype(F32)
    total = slots[0]
    for position in range(1, slots.shape[0]):
        total += slots[position]
    for position in range(out_ref.shape[0]):
        out_ref[position] = total.astype(BF16)


def picks_kernel(core_ref, neighbors_ref, seeds_ref, spread_ref, pick_ref):
    fanout, seeds = neighbors_ref.shape
    rows = spread_ref.shape[0]
    step = lax.broadcasted_iota(jnp.int32, (rows, seeds), 0)
    half = rows // 2
    first = step // half
    lane = step % 128
    side = jnp.where(first == 0, core_ref[0], 1 - core_ref[0])
    row_of = ((step % half) // 128) * 256 + side * 128 + lane
    counts = jnp.zeros((rows, seeds), F32)
    for entry in range(fanout):
        counts += (row_of == neighbors_ref[entry : entry + 1, :]).astype(F32)
    own = (row_of == seeds_ref[...]).astype(F32)
    spread_ref[:, :seeds] = counts.astype(BF16)
    spread_ref[:, seeds:] = own.astype(BF16)
    pick_ref[:seeds] = counts.T.astype(BF16)
    pick_ref[seeds:] = own.T.astype(BF16)


def activate(pre_ref, hidden_shape):
    pre_one = pre_ref[...].reshape(hidden_shape).astype(F32)
    sigmoid = jax.nn.sigmoid(pre_one)
    hidden = (pre_one * sigmoid).astype(BF16)
    return hidden, sigmoid * (1.0 + pre_one * (1.0 - sigmoid))


def mine_kernel(pre_ref, pick_ref, gathered_ref, slope_ref):
    half = slope_ref.shape[0]
    hidden, slope = activate(pre_ref, slope_ref.shape)
    gathered_ref[...] = contract(pick_ref[:, :half], hidden, 1, 0)
    slope_ref[...] = slope


def step_kernel(
    feat_ref,
    pre_ref,
    gathered_ref,
    slope_ref,
    pick_ref,
    spread_ref,
    self_ref,
    neigh_ref,
    cotangent_ref,
    targets_ref,
    pack_ref,
    mine_ref,
    other_ref,
    output_ref,
    grads_ref,
    gathered,
    scratch,
):
    seeds = cotangent_ref.shape[0]
    columns = targets_ref.shape[0]
    half = slope_ref.shape[0]
    hidden, slope_other = activate(pre_ref, slope_ref.shape)
    gathered[...] = contract(pick_ref[:, half:], hidden, 1, 0)
    picked = gathered_ref[...] + gathered[...]
    nbr_mean = (picked[:seeds] / FAN).astype(BF16)
    own = picked[seeds:].astype(BF16)
    pre_two = contract(own, self_ref[...], 1, 0) + contract(nbr_mean, neigh_ref[...], 1, 0)
    gate = jax.nn.sigmoid(pre_two)
    output_ref[...] = (pre_two * gate).astype(BF16)
    slope_two = (
        cotangent_ref[...].astype(F32) * (gate * (1.0 + pre_two * (1.0 - gate)))
    ).astype(BF16)

    scratch[0] = contract(own, slope_two, 0, 0)
    scratch[1] = contract(nbr_mean, slope_two, 0, 0)

    back = jnp.concatenate(
        [contract(slope_two, neigh_ref[...], 1, 1) / FAN, contract(slope_two, self_ref[...], 1, 1)],
        axis=0,
    )
    back_high = back.astype(BF16)
    back_low = (back - back_high.astype(F32)).astype(BF16)
    spread = spread_ref[...]
    back_hidden = contract(spread, back_high, 1, 0) + contract(spread, back_low, 1, 0)
    slope_one = jnp.concatenate(
        [
            (back_hidden[:half] * slope_ref[...]).astype(BF16),
            (back_hidden[half:] * slope_other).astype(BF16),
        ],
        axis=0,
    )
    inputs = jnp.concatenate(
        [
            jnp.concatenate([targets_ref[...], pack_ref[:columns]], axis=1),
            jnp.concatenate([mine_ref[...], other_ref[...]], axis=1),
        ],
        axis=0,
    )
    grad_one = contract(inputs, slope_one, 1, 0).astype(BF16)
    part_rows = (grads_ref.shape[1] - 2 * columns) // 4
    first = pl.multiple_of(feat_ref[0] * part_rows, part_rows)
    grad_two = jnp.concatenate(
        [scratch[0, pl.ds(first, part_rows), :], scratch[1, pl.ds(first, part_rows), :]], axis=0
    )
    two_high = grad_two.astype(BF16)
    two_low = (grad_two - two_high.astype(F32)).astype(BF16)
    every = jnp.concatenate([grad_one, two_high, two_low], axis=0)
    for position in range(grads_ref.shape[0]):
        grads_ref[position] = every


def grads_kernel(parts_ref, one_ref, two_ref):
    total = parts_ref[0].astype(F32)
    for position in range(1, parts_ref.shape[0]):
        total += parts_ref[position].astype(F32)
    columns, part_rows = one_ref.shape[1], two_ref.shape[1]
    one_ref[0] = total[:columns]
    one_ref[1] = total[columns : 2 * columns]
    two = total[2 * columns : 2 * columns + 2 * part_rows] + total[2 * columns + 2 * part_rows :]
    two_ref[0] = two[:part_rows]
    two_ref[1] = two[part_rows:]


def run(kernel, outs, operands, scratch=(), limit=8, flops=0, specs=None):
    shapes = [jax.ShapeDtypeStruct(shape, dtype) for shape, dtype in outs]
    moved = sum(x.size * x.dtype.itemsize for x in operands) + sum(
        x.size * x.dtype.itemsize for x in shapes
    )
    if specs is None:
        specs = [SMEM if x.dtype == jnp.int32 and x.size == 1 else VMEM for x in operands]
    results = pl.pallas_call(
        kernel,
        out_shape=shapes,
        in_specs=specs,
        out_specs=[VMEM] * len(shapes),
        scratch_shapes=list(scratch),
        cost_estimate=pl.CostEstimate(flops=flops, bytes_accessed=moved, transcendentals=0),
        compiler_params=pltpu.CompilerParams(vmem_limit_bytes=limit * MIB),
    )(*operands)
    return results[0] if len(shapes) == 1 else results


def per_device(
    features,
    target_feats,
    tile_values,
    tile_index,
    tile_count,
    self_weight1,
    neigh_weight1,
    self_weight2,
    neigh_weight2,
    neighbors,
    seed_index,
    cotangent,
):
    src_rows, columns = features.shape
    tgt_rows = target_feats.shape[0]
    slots, block, _ = tile_values.shape
    hsize = self_weight2.shape[0]
    seeds = seed_index.shape[0]
    owners = lax.axis_size(NODE)
    near, far = lax.axis_size("zl"), lax.axis_size("zh")
    part_rows = hsize // lax.axis_size(FEAT)
    all_blocks = tgt_rows * owners // block
    half = tgt_rows // 2
    span = half // near
    core = lax.axis_index("c").reshape(1)
    feat = lax.axis_index(FEAT).reshape(1)
    halves = pltpu.VMEM((near, 2, columns, block), BF16)
    swap = [(0, 1), (1, 0)]

    with jax.named_scope("aggregate_tiles"):
        aggregate = run(
            aggregate_kernel,
            [((all_blocks, columns, block), BF16)],
            (tile_count, tile_index.T, tile_values, features.T),
            [
                pltpu.VMEM(tile_values.shape, BF16),
                pltpu.VMEM((columns, src_rows), BF16),
                pltpu.VMEM((src_rows // block, columns, block), BF16),
                pltpu.VMEM((slots, columns, block), F32),
                pltpu.VMEM((all_blocks, columns, block), F32),
                pltpu.SemaphoreType.DMA((4,)),
                pltpu.SemaphoreType.DMA,
            ],
            limit=56,
            specs=[SMEM, SMEM, HBM, HBM],
        )
    with jax.named_scope("aggregate_exchange"):
        parts = lax.all_to_all(
            aggregate.reshape(owners, tgt_rows // block * columns, block), NODE, 0, 0, tiled=True
        )
    with jax.named_scope("inputs_exchange"):
        targets_mine, pack = run(
            pack_kernel,
            [((columns, half), BF16), ((2 * columns, half), BF16)],
            (core, target_feats.T, self_weight1, neigh_weight1),
            [halves],
        )
        pack_other = lax.ppermute(pack, "c", swap)
    with jax.named_scope("owned_sum"):
        agg_mine, agg_other = run(
            owned_kernel,
            [((columns, half), BF16), ((columns, half), BF16)],
            (core, parts),
            [halves],
        )
        agg_arrived = lax.ppermute(agg_other, "c", swap)
    with jax.named_scope("partial_pre"):
        pieces = run(
            partial_kernel,
            [((near, span, hsize), BF16)],
            (targets_mine, pack_other, agg_mine, agg_arrived, self_weight1, neigh_weight1),
        )
    with jax.named_scope("pre_sum_near"):
        pieces = lax.all_to_all(pieces, "zl", 0, 0, tiled=True)
        quarter = run(near_kernel, [((span, hsize), BF16)], (pieces,))
    with jax.named_scope("picks"):
        spread, pick = run(
            picks_kernel,
            [((tgt_rows, 2 * seeds), BF16), ((2 * seeds, tgt_rows), BF16)],
            (core, neighbors.T, seed_index.reshape(1, -1)),
            limit=16,
            flops=20 * tgt_rows * seeds,
        )
    with jax.named_scope("pre_sum_far"):
        arrived = [
            lax.ppermute(quarter, "zh", [(i, (i + step) % far) for i in range(far)])
            for step in (2, 1, 3)
        ]
        copies = run(
            far_kernel,
            [((near, span, hsize), BF16)],
            (lax.axis_index("zh").reshape(1), quarter, *arrived, pick),
            [pltpu.VMEM((far, span, hsize), F32)],
            specs=[SMEM] + [VMEM] * 4 + [ANY],
        )
    with jax.named_scope("pre_gather"):
        pre_mine = lax.all_to_all(copies, "zl", 0, 0, tiled=True)
        pre_other = lax.ppermute(pre_mine, "c", swap)
    with jax.named_scope("step_mine"):
        gathered, slope = run(
            mine_kernel,
            [((2 * seeds, hsize), F32), ((half, hsize), F32)],
            (pre_mine, pick),
            limit=12,
            flops=4 * seeds * half * hsize,
        )
    with jax.named_scope("step"):
        output, grads = run(
            step_kernel,
            [(cotangent.shape, BF16), ((owners, 2 * columns + 4 * part_rows, hsize), BF16)],
            (
                feat,
                pre_other,
                gathered,
                slope,
                pick,
                spread,
                self_weight2,
                neigh_weight2,
                cotangent,
                targets_mine,
                pack,
                agg_mine,
                agg_other,
            ),
            [pltpu.VMEM((2 * seeds, hsize), F32), pltpu.VMEM((2, hsize, hsize), F32)],
            limit=24,
        )
    with jax.named_scope("grad_sum"):
        grads = lax.all_to_all(grads, NODE, 0, 0, tiled=True)
        grad_one, grad_two = run(
            grads_kernel,
            [((2, columns, hsize), F32), ((2, part_rows, hsize), F32)],
            (grads,),
        )
    return (output, grad_one, grad_two)


def solution(mesh):
    fine = Mesh(mesh.devices.reshape(4, 4, 2, 4, 4), FEAT + NODE)
    placed = (
        P(NODE, FEAT),
        P(NODE, FEAT),
        P(NODE, None, None),
        P(NODE, None),
        P(NODE),
        P(FEAT, None),
        P(FEAT, None),
        P(),
        P(),
        P(NODE, None),
        P(NODE),
        P(NODE, None),
    )
    return jax.shard_map(
        per_device,
        mesh=fine,
        in_specs=placed,
        out_specs=(P(NODE, None), P(None, FEAT, None), P(None, FEAT, None)),
        check_vma=False,
    )
```

```python
import functools

import jax
import jax.numpy as jnp
from jax import lax
from jax.experimental import pallas as pl
from jax.experimental.pallas import tpu as pltpu
from jax.sharding import Mesh
from jax.sharding import PartitionSpec as P

BF16 = jnp.bfloat16
F32 = jnp.float32
NODE = ("x", "y")
FEAT = ("zh", "zl", "c")
FAN = 10
MIB = 1 << 20

VMEM = pl.BlockSpec(memory_space=pltpu.VMEM)
HBM = pl.BlockSpec(memory_space=pltpu.HBM)
ANY = pl.BlockSpec(memory_space=pl.ANY)
SMEM = pl.BlockSpec(memory_space=pltpu.SMEM)


def contract(left, right, left_dim, right_dim):
    return lax.dot_general(
        left, right, (((left_dim,), (right_dim,)), ((), ())), preferred_element_type=F32
    )


def aggregate_kernel(owners, near, count_ref, index_ref, tiles_ref, feats_ref, out_ref, sources, products, total):
    slots, block, _ = tiles_ref.shape
    for position in range(sources.shape[0]):
        sources[position] = feats_ref[:, position * block : (position + 1) * block]
    out_ref[...] = jnp.zeros_like(out_ref)
    places = []
    for slot in range(slots):
        target = index_ref[0, slot]
        place = ((target & 1) * owners + (target >> 3)) * near + ((target & 7) >> 1)
        places.append(place)
        total[place] = jnp.zeros(total.shape[1:], F32)
    live_tiles = count_ref[...]
    for slot in range(slots):
        in_use = (slot < live_tiles).astype(F32)
        products[slot] = contract(sources[index_ref[1, slot]], tiles_ref[slot], 1, 1) * in_use
    for slot in range(slots):
        total[places[slot]] += products[slot]
    for slot in range(slots):
        out_ref[places[slot]] = total[places[slot]].astype(BF16)


def split_blocks(core, halves, mine_ref, other_ref):
    block = halves.shape[3]
    for position in range(halves.shape[0]):
        span = slice(position * block, (position + 1) * block)
        mine_ref[:, span] = halves[position, core]
        other_ref[:, span] = halves[position, 1 - core]


def pack_kernel(core_ref, targets_ref, self_ref, neigh_ref, mine_ref, pack_ref, halves):
    columns = targets_ref.shape[0]
    near, _, _, block = halves.shape
    for position in range(2 * near):
        halves[position // 2, position % 2] = targets_ref[:, position * block : (position + 1) * block]
    split_blocks(core_ref[0], halves, mine_ref, pack_ref.at[:columns])
    hsize = self_ref.shape[1]
    pack_ref[columns:, :hsize] = self_ref[...]
    pack_ref[columns:, hsize:] = neigh_ref[...]


def partial_kernel(
    core_ref, near_ref, parts_ref, targets_ref, pack_ref, self_ref, neigh_ref,
    out_ref, own_ref, mine_ref, other_ref, owned, total
):
    columns, hsize = self_ref.shape
    block = parts_ref.shape[2]
    owners = parts_ref.shape[0] // 2
    for side in range(2):
        block_sum = parts_ref[side * owners].astype(F32)
        for source in range(1, owners):
            block_sum += parts_ref[side * owners + source].astype(F32)
        block_sum = block_sum.astype(BF16)
        for position in range(block_sum.shape[0] // columns):
            owned[side, :, position * block : (position + 1) * block] = block_sum[
                position * columns : (position + 1) * columns
            ]
    core = core_ref[0]
    mine_ref[...] = owned[core]
    other_ref[...] = owned[1 - core]
    inputs = jnp.concatenate(
        [targets_ref[...], pack_ref[:columns], mine_ref[...], other_ref[...]], axis=0
    )
    weights = jnp.concatenate(
        [self_ref[...], pack_ref[columns:, :hsize], neigh_ref[...], pack_ref[columns:, hsize:]], axis=0
    )
    total[...] = contract(inputs, weights, 0, 0).reshape(total.shape)
    out_ref[...] = total[...].astype(BF16)
    own_ref[...] = total[near_ref[0]]


def near_kernel(near_ref, own_ref, parts_ref, agg_ref, out_ref):
    near = near_ref[0]
    total = own_ref[...]
    for position in range(1, parts_ref.shape[0]):
        total += parts_ref[(near + position) & (parts_ref.shape[0] - 1)].astype(F32)
    out_ref[...] = total.astype(BF16)


def far_kernel(far_ref, own_ref, one_ref, three_ref, two_ref, picks_ref, out_ref, slots):
    far = far_ref[0]
    slots[far] = own_ref[...].astype(F32)
    for step, ref in ((2, two_ref), (1, one_ref), (3, three_ref)):
        slots[lax.rem(far + slots.shape[0] - step, slots.shape[0])] = ref[...].astype(F32)
    total = slots[0]
    for position in range(1, slots.shape[0]):
        total += slots[position]
    for position in range(out_ref.shape[0]):
        out_ref[position] = total.astype(BF16)


def picks_kernel(core_ref, neighbors_ref, seeds_ref, spread_ref, pick_ref):
    fanout, seeds = neighbors_ref.shape
    rows = spread_ref.shape[0]
    step = lax.broadcasted_iota(jnp.int32, (rows, seeds), 0)
    half = rows // 2
    first = step // half
    lane = step % 128
    side = jnp.where(first == 0, core_ref[0], 1 - core_ref[0])
    row_of = ((step % half) // 128) * 256 + side * 128 + lane
    counts = jnp.zeros((rows, seeds), F32)
    for entry in range(fanout):
        counts += (row_of == neighbors_ref[entry : entry + 1, :]).astype(F32)
    own = (row_of == seeds_ref[...]).astype(F32)
    spread_ref[:, :seeds] = counts.astype(BF16)
    spread_ref[:, seeds:] = own.astype(BF16)
    pick_ref[:seeds] = counts.T.astype(BF16)
    pick_ref[seeds:] = own.T.astype(BF16)


def activate(pre_ref, hidden_shape):
    pre_one = pre_ref[...].reshape(hidden_shape).astype(F32)
    sigmoid = jax.nn.sigmoid(pre_one)
    hidden = (pre_one * sigmoid).astype(BF16)
    return hidden, sigmoid * (1.0 + pre_one * (1.0 - sigmoid))


def mine_kernel(pre_ref, pick_ref, gathered_ref, slope_ref):
    half = slope_ref.shape[0]
    hidden, slope = activate(pre_ref, slope_ref.shape)
    gathered_ref[...] = contract(pick_ref[:, :half], hidden, 1, 0)
    slope_ref[...] = slope


def step_kernel(
    feat_ref,
    pre_ref,
    gathered_ref,
    slope_ref,
    pick_ref,
    spread_ref,
    self_ref,
    neigh_ref,
    cotangent_ref,
    targets_ref,
    pack_ref,
    mine_ref,
    other_ref,
    output_ref,
    grads_ref,
    gathered,
    scratch,
    output,
    output_sem,
):
    seeds = cotangent_ref.shape[0]
    columns = targets_ref.shape[0]
    half = slope_ref.shape[0]
    hidden, slope_other = activate(pre_ref, slope_ref.shape)
    gathered[...] = contract(pick_ref[:, half:], hidden, 1, 0)
    picked = gathered_ref[...] + gathered[...]
    nbr_mean = (picked[:seeds] / FAN).astype(BF16)
    own = picked[seeds:].astype(BF16)
    pre_two = contract(own, self_ref[...], 1, 0) + contract(nbr_mean, neigh_ref[...], 1, 0)
    gate = jax.nn.sigmoid(pre_two)
    output[...] = (pre_two * gate).astype(BF16)
    copy = pltpu.make_async_copy(output, output_ref, output_sem)
    copy.start()
    slope_two = (
        cotangent_ref[...].astype(F32) * (gate * (1.0 + pre_two * (1.0 - gate)))
    ).astype(BF16)

    scratch[0] = contract(own, slope_two, 0, 0)
    scratch[1] = contract(nbr_mean, slope_two, 0, 0)

    back = jnp.concatenate(
        [contract(slope_two, neigh_ref[...], 1, 1) / FAN, contract(slope_two, self_ref[...], 1, 1)],
        axis=0,
    )
    back_high = back.astype(BF16)
    back_low = (back - back_high.astype(F32)).astype(BF16)
    spread = spread_ref[...]
    back_hidden = contract(spread, back_high, 1, 0) + contract(spread, back_low, 1, 0)
    slope_one = jnp.concatenate(
        [
            (back_hidden[:half] * slope_ref[...]).astype(BF16),
            (back_hidden[half:] * slope_other).astype(BF16),
        ],
        axis=0,
    )
    inputs = jnp.concatenate(
        [
            jnp.concatenate([targets_ref[...], pack_ref[:columns]], axis=1),
            jnp.concatenate([mine_ref[...], other_ref[...]], axis=1),
        ],
        axis=0,
    )
    grad_one = contract(inputs, slope_one, 1, 0).astype(BF16)
    part_rows = (grads_ref.shape[1] - 2 * columns) // 4
    first = pl.multiple_of(feat_ref[0] * part_rows, part_rows)
    grad_two = jnp.concatenate(
        [scratch[0, pl.ds(first, part_rows), :], scratch[1, pl.ds(first, part_rows), :]], axis=0
    )
    two_high = grad_two.astype(BF16)
    two_low = (grad_two - two_high.astype(F32)).astype(BF16)
    every = jnp.concatenate([grad_one, two_high, two_low], axis=0)
    for position in range(grads_ref.shape[0]):
        grads_ref[position] = every
    copy.wait()


def grads_kernel(parts_ref, one_ref, two_ref):
    total = parts_ref[0].astype(F32)
    for position in range(1, parts_ref.shape[0]):
        total += parts_ref[position].astype(F32)
    columns, part_rows = one_ref.shape[1], two_ref.shape[1]
    one_ref[0] = total[:columns]
    one_ref[1] = total[columns : 2 * columns]
    two = total[2 * columns : 2 * columns + 2 * part_rows] + total[2 * columns + 2 * part_rows :]
    two_ref[0] = two[:part_rows]
    two_ref[1] = two[part_rows:]


def run(kernel, outs, operands, scratch=(), limit=8, flops=0, specs=None, out_specs=None):
    shapes = [jax.ShapeDtypeStruct(shape, dtype) for shape, dtype in outs]
    moved = sum(x.size * x.dtype.itemsize for x in operands) + sum(
        x.size * x.dtype.itemsize for x in shapes
    )
    if specs is None:
        specs = [SMEM if x.dtype == jnp.int32 and x.size == 1 else VMEM for x in operands]
    results = pl.pallas_call(
        kernel,
        out_shape=shapes,
        in_specs=specs,
        out_specs=out_specs or [VMEM] * len(shapes),
        scratch_shapes=list(scratch),
        cost_estimate=pl.CostEstimate(flops=flops, bytes_accessed=moved, transcendentals=0),
        compiler_params=pltpu.CompilerParams(vmem_limit_bytes=limit * MIB),
    )(*operands)
    return results[0] if len(shapes) == 1 else results


def per_device(
    features,
    target_feats,
    tile_values,
    tile_index,
    tile_count,
    self_weight1,
    neigh_weight1,
    self_weight2,
    neigh_weight2,
    neighbors,
    seed_index,
    cotangent,
):
    src_rows, columns = features.shape
    tgt_rows = target_feats.shape[0]
    slots, block, _ = tile_values.shape
    hsize = self_weight2.shape[0]
    seeds = seed_index.shape[0]
    owners = lax.axis_size(NODE)
    near, far = lax.axis_size("zl"), lax.axis_size("zh")
    part_rows = hsize // lax.axis_size(FEAT)
    all_blocks = tgt_rows * owners // block
    half = tgt_rows // 2
    span = half // near
    core = lax.axis_index("c").reshape(1)
    feat = lax.axis_index(FEAT).reshape(1)
    halves = pltpu.VMEM((near, 2, columns, block), BF16)
    position = lax.axis_index("zl").reshape(1)
    swap = [(0, 1), (1, 0)]

    with jax.named_scope("aggregate_tiles"):
        aggregate = run(
            functools.partial(aggregate_kernel, owners, near),
            [((all_blocks, columns, block), BF16)],
            (tile_count.reshape(1, 1), tile_index.T, tile_values, features.T),
            [
                pltpu.VMEM((src_rows // block, columns, block), BF16),
                pltpu.VMEM((slots, columns, block), F32),
                pltpu.VMEM((all_blocks, columns, block), F32),
            ],
            limit=56,
            specs=[VMEM, SMEM, VMEM, VMEM],
        )
    with jax.named_scope("aggregate_exchange"):
        parts = lax.all_to_all(
            aggregate.reshape(2 * owners, near * columns, block), ("c",) + NODE, 0, 0, tiled=True
        )
    with jax.named_scope("inputs_exchange"):
        targets_mine, pack = run(
            pack_kernel,
            [((columns, half), BF16), ((2 * columns, half), BF16)],
            (core, target_feats.T, self_weight1, neigh_weight1),
            [halves],
        )
        pack_other = lax.ppermute(pack, "c", swap)
    with jax.named_scope("partial_pre"):
        pieces, own, agg_mine, agg_send = run(
            partial_kernel,
            [((near, span, hsize), BF16), ((span, hsize), F32), ((columns, half), BF16), ((columns, half), BF16)],
            (core, position, parts, targets_mine, pack_other, self_weight1, neigh_weight1),
            [pltpu.VMEM((2, columns, half), BF16), pltpu.VMEM((near, span, hsize), F32)],
        )
        agg_other = lax.ppermute(agg_send, "c", swap)
    with jax.named_scope("pre_sum_near"):
        pieces = lax.all_to_all(pieces, "zl", 0, 0, tiled=True)
        quarter = run(near_kernel, [((span, hsize), BF16)], (position, own, pieces, agg_other), specs=[SMEM, VMEM, VMEM, ANY])
    with jax.named_scope("picks"):
        spread, pick = run(
            picks_kernel,
            [((tgt_rows, 2 * seeds), BF16), ((2 * seeds, tgt_rows), BF16)],
            (core, neighbors.T, seed_index.reshape(1, -1)),
            limit=16,
            flops=20 * tgt_rows * seeds,
        )
    with jax.named_scope("pre_sum_far"):
        arrived = [
            lax.ppermute(quarter, "zh", [(i, (i + step) % far) for i in range(far)])
            for step in (1, 3, 2)
        ]
        copies = run(
            far_kernel,
            [((near, span, hsize), BF16)],
            (lax.axis_index("zh").reshape(1), quarter, *arrived, pick),
            [pltpu.VMEM((far, span, hsize), F32)],
            specs=[SMEM] + [VMEM] * 4 + [ANY],
        )
    with jax.named_scope("pre_gather"):
        pre_mine = lax.all_to_all(copies, "zl", 0, 0, tiled=True)
        pre_other = lax.ppermute(pre_mine, "c", swap)
    with jax.named_scope("step_mine"):
        gathered, slope = run(
            mine_kernel,
            [((2 * seeds, hsize), F32), ((half, hsize), F32)],
            (pre_mine, pick),
            limit=12,
            flops=4 * seeds * half * hsize,
        )
    with jax.named_scope("step"):
        output, grads = run(
            step_kernel,
            [(cotangent.shape, BF16), ((owners, 2 * columns + 4 * part_rows, hsize), BF16)],
            (
                feat,
                pre_other,
                gathered,
                slope,
                pick,
                spread,
                self_weight2,
                neigh_weight2,
                cotangent,
                targets_mine,
                pack,
                agg_mine,
                agg_other,
            ),
            [
                pltpu.VMEM((2 * seeds, hsize), F32),
                pltpu.VMEM((2, hsize, hsize), F32),
                pltpu.VMEM(cotangent.shape, BF16),
                pltpu.SemaphoreType.DMA,
            ],
            limit=24,
            out_specs=[HBM, VMEM],
        )
    with jax.named_scope("grad_sum"):
        grads = lax.all_to_all(grads, NODE, 0, 0, tiled=True)
        grad_one, grad_two = run(
            grads_kernel,
            [((2, columns, hsize), F32), ((2, part_rows, hsize), F32)],
            (grads,),
        )
    return (output, grad_one, grad_two)


def solution(mesh):
    fine = Mesh(mesh.devices.reshape(4, 4, 2, 4, 4), FEAT + NODE)
    placed = (
        P(NODE, FEAT),
        P(NODE, FEAT),
        P(NODE, None, None),
        P(NODE, None),
        P(NODE),
        P(FEAT, None),
        P(FEAT, None),
        P(),
        P(),
        P(NODE, None),
        P(NODE),
        P(NODE, None),
    )
    return jax.shard_map(
        per_device,
        mesh=fine,
        in_specs=placed,
        out_specs=(P(NODE, None), P(None, FEAT, None), P(None, FEAT, None)),
        check_vma=False,
    )
```

```python
import jax
import jax.numpy as jnp
from jax import lax
from jax.experimental import pallas as pl
from jax.experimental.pallas import tpu as pltpu
from jax.sharding import Mesh
from jax.sharding import PartitionSpec as P

BF16 = jnp.bfloat16
F32 = jnp.float32
NODE = ("x", "y")
FEAT = ("zh", "zl", "c")
NEAR = ("zl", "c")
FAN = 10
MIB = 1 << 20

VMEM = pl.BlockSpec(memory_space=pltpu.VMEM)
HBM = pl.BlockSpec(memory_space=pltpu.HBM)
ANY = pl.BlockSpec(memory_space=pl.ANY)
SMEM = pl.BlockSpec(memory_space=pltpu.SMEM)


def contract(left, right, left_dim, right_dim):
    return lax.dot_general(
        left, right, (((left_dim,), (right_dim,)), ((), ())), preferred_element_type=F32
    )


def aggregate_kernel(count_ref, index_ref, tiles_ref, feats_ref, out_ref, sources, products, total):
    slots, block, _ = tiles_ref.shape
    for position in range(sources.shape[0]):
        sources[position] = feats_ref[:, position * block : (position + 1) * block]
    out_ref[...] = jnp.zeros_like(out_ref)
    places = []
    for slot in range(slots):
        place = index_ref[0, slot]
        places.append(place)
        total[place] = jnp.zeros(total.shape[1:], F32)
    live_tiles = count_ref[...]
    for slot in range(slots):
        in_use = (slot < live_tiles).astype(F32)
        products[slot] = contract(sources[index_ref[1, slot]], tiles_ref[slot], 1, 1) * in_use
    for slot in range(slots):
        total[places[slot]] += products[slot]
    for slot in range(slots):
        out_ref[places[slot]] = total[places[slot]].astype(BF16)


def split_blocks(core, halves, mine_ref, other_ref):
    block = halves.shape[3]
    for position in range(halves.shape[0]):
        span = slice(position * block, (position + 1) * block)
        mine_ref[:, span] = halves[position, core]
        other_ref[:, span] = halves[position, 1 - core]


def pack_kernel(core_ref, targets_ref, self_ref, neigh_ref, pack_ref, mine_ref, other_ref, halves):
    near, _, columns, block = halves.shape
    for position in range(2 * near):
        halves[position // 2, position % 2] = targets_ref[:, position * block : (position + 1) * block]
    split_blocks(core_ref[0], halves, mine_ref, other_ref)
    hsize = self_ref.shape[1]
    pack_ref[:columns] = other_ref[...]
    pack_ref[columns:, :hsize] = self_ref[...]
    pack_ref[columns:, hsize:] = neigh_ref[...]


def pieces_kernel(near_ref, targets_ref, pack_ref, arrived_ref, *rest):
    piece_refs, pieces = rest[:-1], rest[-1]
    near, columns, block = pieces.shape[0], targets_ref.shape[0], pieces.shape[2]
    for position in range(near):
        span = slice(position * block, (position + 1) * block)
        pieces[position, :columns] = targets_ref[:, span]
        pieces[position, columns:] = arrived_ref[:columns, span]
    for step, ref in enumerate(piece_refs):
        ref[:, :block] = pieces[(near_ref[0] + step) & (near - 1)]
        ref[:columns, block:] = pack_ref[columns:]
        ref[columns:, block:] = arrived_ref[columns:]


def owned_kernel(core_ref, parts_ref, one_ref, two_ref, three_ref, blocks_ref, mine_ref, other_ref, halves):
    near, _, columns, _ = halves.shape
    for position in range(2 * near):
        span = slice(position * columns, (position + 1) * columns)
        block = parts_ref[0, span].astype(F32)
        for source in range(1, parts_ref.shape[0]):
            block += parts_ref[source, span].astype(F32)
        block = block.astype(BF16)
        blocks_ref[position] = block
        halves[position // 2, position % 2] = block
    split_blocks(core_ref[0], halves, mine_ref, other_ref)


def partial_kernel(core_ref, near_ref, blocks_ref, *rest):
    piece_refs, (out_ref, inputs, weights, sides) = rest[:-4], rest[-4:]
    group, columns, block = blocks_ref.shape
    near, hsize = len(piece_refs), out_ref.shape[1]
    core = core_ref[0]
    for step, ref in enumerate(piece_refs):
        span = slice(step * 2 * columns, (step + 1) * 2 * columns)
        inputs[span] = ref[:, :block]
        weights[span] = ref[:, block : block + hsize]
        source = (near_ref[0] + near - step) & (near - 1)
        sides[source, core] = ref[:columns, block + hsize :]
        sides[source, 1 - core] = ref[columns:, block + hsize :]
    for position in range(group):
        span = slice((group + position) * columns, (group + position + 1) * columns)
        inputs[span] = blocks_ref[position]
        weights[span] = sides[position // 2, position % 2]
    out_ref[...] = contract(inputs[...], weights[...], 0, 0).astype(BF16)


def far_kernel(far_ref, own_ref, one_ref, three_ref, two_ref, picks_ref, out_ref, slots):
    far = far_ref[0]
    slots[far] = own_ref[...].astype(F32)
    for step, ref in ((2, two_ref), (1, one_ref), (3, three_ref)):
        slots[lax.rem(far + slots.shape[0] - step, slots.shape[0])] = ref[...].astype(F32)
    total = slots[0]
    for position in range(1, slots.shape[0]):
        total += slots[position]
    for position in range(out_ref.shape[0]):
        out_ref[position] = total.astype(BF16)


def picks_kernel(core_ref, neighbors_ref, seeds_ref, spread_ref, pick_ref):
    fanout, seeds = neighbors_ref.shape
    rows = spread_ref.shape[0]
    step = lax.broadcasted_iota(jnp.int32, (rows, seeds), 0)
    half = rows // 2
    first = step // half
    lane = step % 128
    side = jnp.where(first == 0, core_ref[0], 1 - core_ref[0])
    row_of = ((step % half) // 128) * 256 + side * 128 + lane
    counts = jnp.zeros((rows, seeds), F32)
    for entry in range(fanout):
        counts += (row_of == neighbors_ref[entry : entry + 1, :]).astype(F32)
    own = (row_of == seeds_ref[...]).astype(F32)
    spread_ref[:, :seeds] = counts.astype(BF16)
    spread_ref[:, seeds:] = own.astype(BF16)
    pick_ref[:seeds] = counts.T.astype(BF16)
    pick_ref[seeds:] = own.T.astype(BF16)


def activate(pre_ref, hidden_shape):
    pre_one = pre_ref[...].reshape(hidden_shape).astype(F32)
    sigmoid = jax.nn.sigmoid(pre_one)
    hidden = (pre_one * sigmoid).astype(BF16)
    return hidden, sigmoid * (1.0 + pre_one * (1.0 - sigmoid))


def mine_kernel(pre_ref, pick_ref, gathered_ref, slope_ref):
    half = slope_ref.shape[0]
    hidden, slope = activate(pre_ref, slope_ref.shape)
    gathered_ref[...] = contract(pick_ref[:, :half], hidden, 1, 0)
    slope_ref[...] = slope


def step_kernel(
    feat_ref,
    pre_ref,
    gathered_ref,
    slope_ref,
    pick_ref,
    spread_ref,
    self_ref,
    neigh_ref,
    cotangent_ref,
    targets_ref,
    targets_other_ref,
    mine_ref,
    other_ref,
    output_ref,
    grads_ref,
    gathered,
    scratch,
    output,
    output_sem,
):
    seeds = cotangent_ref.shape[0]
    columns = targets_ref.shape[0]
    half = slope_ref.shape[0]
    hidden, slope_other = activate(pre_ref, slope_ref.shape)
    gathered[...] = contract(pick_ref[:, half:], hidden, 1, 0)
    picked = gathered_ref[...] + gathered[...]
    nbr_mean = (picked[:seeds] / FAN).astype(BF16)
    own = picked[seeds:].astype(BF16)
    pre_two = contract(own, self_ref[...], 1, 0) + contract(nbr_mean, neigh_ref[...], 1, 0)
    gate = jax.nn.sigmoid(pre_two)
    output[...] = (pre_two * gate).astype(BF16)
    copy = pltpu.make_async_copy(output, output_ref, output_sem)
    copy.start()
    slope_two = (
        cotangent_ref[...].astype(F32) * (gate * (1.0 + pre_two * (1.0 - gate)))
    ).astype(BF16)

    scratch[0] = contract(own, slope_two, 0, 0)
    scratch[1] = contract(nbr_mean, slope_two, 0, 0)

    back = jnp.concatenate(
        [contract(slope_two, neigh_ref[...], 1, 1) / FAN, contract(slope_two, self_ref[...], 1, 1)],
        axis=0,
    )
    back_high = back.astype(BF16)
    back_low = (back - back_high.astype(F32)).astype(BF16)
    spread = spread_ref[...]
    back_hidden = contract(spread, back_high, 1, 0) + contract(spread, back_low, 1, 0)
    slope_one = jnp.concatenate(
        [
            (back_hidden[:half] * slope_ref[...]).astype(BF16),
            (back_hidden[half:] * slope_other).astype(BF16),
        ],
        axis=0,
    )
    inputs = jnp.concatenate(
        [
            jnp.concatenate([targets_ref[...], targets_other_ref[...]], axis=1),
            jnp.concatenate([mine_ref[...], other_ref[...]], axis=1),
        ],
        axis=0,
    )
    grad_one = contract(inputs, slope_one, 1, 0).astype(BF16)
    part_rows = (grads_ref.shape[1] - 2 * columns) // 2
    first = pl.multiple_of(feat_ref[0] * part_rows, part_rows)
    grad_two = jnp.concatenate(
        [scratch[0, pl.ds(first, part_rows), :], scratch[1, pl.ds(first, part_rows), :]], axis=0
    )
    every = jnp.concatenate([grad_one, grad_two.astype(BF16)], axis=0)
    for position in range(grads_ref.shape[0]):
        grads_ref[position] = every
    copy.wait()


def grads_kernel(parts_ref, one_ref, two_ref):
    total = parts_ref[0].astype(F32)
    for position in range(1, parts_ref.shape[0]):
        total += parts_ref[position].astype(F32)
    columns, part_rows = one_ref.shape[1], two_ref.shape[1]
    one_ref[0] = total[:columns]
    one_ref[1] = total[columns : 2 * columns]
    two_ref[0] = total[2 * columns : 2 * columns + part_rows]
    two_ref[1] = total[2 * columns + part_rows :]


def run(kernel, outs, operands, scratch=(), limit=8, flops=0, specs=None, out_specs=None):
    shapes = [jax.ShapeDtypeStruct(shape, dtype) for shape, dtype in outs]
    moved = sum(x.size * x.dtype.itemsize for x in operands) + sum(
        x.size * x.dtype.itemsize for x in shapes
    )
    if specs is None:
        specs = [SMEM if x.dtype == jnp.int32 and x.size == 1 else VMEM for x in operands]
    results = pl.pallas_call(
        kernel,
        out_shape=shapes,
        in_specs=specs,
        out_specs=out_specs or [VMEM] * len(shapes),
        scratch_shapes=list(scratch),
        cost_estimate=pl.CostEstimate(flops=flops, bytes_accessed=moved, transcendentals=0),
        compiler_params=pltpu.CompilerParams(vmem_limit_bytes=limit * MIB),
    )(*operands)
    return results[0] if len(shapes) == 1 else results


def per_device(
    features,
    target_feats,
    tile_values,
    tile_index,
    tile_count,
    self_weight1,
    neigh_weight1,
    self_weight2,
    neigh_weight2,
    neighbors,
    seed_index,
    cotangent,
):
    src_rows, columns = features.shape
    tgt_rows = target_feats.shape[0]
    slots, block, _ = tile_values.shape
    hsize = self_weight2.shape[0]
    seeds = seed_index.shape[0]
    owners = lax.axis_size(NODE)
    near, far = lax.axis_size("zl"), lax.axis_size("zh")
    part_rows = hsize // lax.axis_size(FEAT)
    all_blocks = tgt_rows * owners // block
    half = tgt_rows // 2
    span = half // near
    core = lax.axis_index("c").reshape(1)
    feat = lax.axis_index(FEAT).reshape(1)
    halves = pltpu.VMEM((near, 2, columns, block), BF16)
    position = lax.axis_index("zl").reshape(1)
    swap = [(0, 1), (1, 0)]

    with jax.named_scope("aggregate_tiles"):
        aggregate = run(
            aggregate_kernel,
            [((all_blocks, columns, block), BF16)],
            (tile_count.reshape(1, 1), tile_index.T, tile_values, features.T),
            [
                pltpu.VMEM((src_rows // block, columns, block), BF16),
                pltpu.VMEM((slots, columns, block), F32),
                pltpu.VMEM((all_blocks, columns, block), F32),
            ],
            limit=56,
            specs=[VMEM, SMEM, VMEM, VMEM],
        )
    with jax.named_scope("aggregate_exchange"):
        parts = lax.all_to_all(
            aggregate.reshape(owners, tgt_rows // block * columns, block), NODE, 0, 0, tiled=True
        )
    with jax.named_scope("inputs_exchange"):
        pack, targets_mine, targets_other = run(
            pack_kernel,
            [((2 * columns, half), BF16), ((columns, half), BF16), ((columns, half), BF16)],
            (core, target_feats.T, self_weight1, neigh_weight1),
            [halves],
        )
        arrived = lax.ppermute(pack, "c", swap)
        sends = run(
            pieces_kernel,
            [((2 * columns, block + 2 * hsize), BF16)] * near,
            (position, targets_mine, pack, arrived),
            [pltpu.VMEM((near, 2 * columns, block), BF16)],
        )
        pieces = [sends[0]] + [
            lax.ppermute(sends[step], "zl", [(i, (i + step) % near) for i in range(near)])
            for step in range(1, near)
        ]
    with jax.named_scope("owned_sum"):
        blocks, agg_mine, agg_other = run(
            owned_kernel,
            [((2 * near, columns, block), BF16), ((columns, half), BF16), ((columns, half), BF16)],
            (core, parts, *pieces[1:]),
            [halves],
            specs=[SMEM, VMEM] + [ANY] * (near - 1),
        )
    with jax.named_scope("near_exchange"):
        blocks = lax.all_to_all(blocks, NEAR, 0, 0, tiled=True)
    with jax.named_scope("partial_pre"):
        quarter = run(
            partial_kernel,
            [((span, hsize), BF16)],
            (core, position, blocks, *pieces),
            [
                pltpu.VMEM((4 * near * columns, span), BF16),
                pltpu.VMEM((4 * near * columns, hsize), BF16),
                pltpu.VMEM((near, 2, columns, hsize), BF16),
            ],
        )
    with jax.named_scope("picks"):
        spread, pick = run(
            picks_kernel,
            [((tgt_rows, 2 * seeds), BF16), ((2 * seeds, tgt_rows), BF16)],
            (core, neighbors.T, seed_index.reshape(1, -1)),
            limit=16,
            flops=20 * tgt_rows * seeds,
        )
    with jax.named_scope("pre_sum_far"):
        arrived = [
            lax.ppermute(quarter, "zh", [(i, (i + step) % far) for i in range(far)])
            for step in (1, 3, 2)
        ]
        copies = run(
            far_kernel,
            [((near, span, hsize), BF16)],
            (lax.axis_index("zh").reshape(1), quarter, *arrived, pick),
            [pltpu.VMEM((far, span, hsize), F32)],
            specs=[SMEM] + [VMEM] * 4 + [ANY],
        )
    with jax.named_scope("pre_gather"):
        pre_mine = lax.all_to_all(copies, "zl", 0, 0, tiled=True)
        pre_other = lax.ppermute(pre_mine, "c", swap)
    with jax.named_scope("step_mine"):
        gathered, slope = run(
            mine_kernel,
            [((2 * seeds, hsize), F32), ((half, hsize), F32)],
            (pre_mine, pick),
            limit=12,
            flops=4 * seeds * half * hsize,
        )
    with jax.named_scope("step"):
        output, grads = run(
            step_kernel,
            [(cotangent.shape, BF16), ((owners, 2 * columns + 2 * part_rows, hsize), BF16)],
            (
                feat,
                pre_other,
                gathered,
                slope,
                pick,
                spread,
                self_weight2,
                neigh_weight2,
                cotangent,
                targets_mine,
                targets_other,
                agg_mine,
                agg_other,
            ),
            [
                pltpu.VMEM((2 * seeds, hsize), F32),
                pltpu.VMEM((2, hsize, hsize), F32),
                pltpu.VMEM(cotangent.shape, BF16),
                pltpu.SemaphoreType.DMA,
            ],
            limit=24,
            out_specs=[HBM, VMEM],
        )
    with jax.named_scope("grad_sum"):
        grads = lax.all_to_all(grads, NODE, 0, 0, tiled=True)
        grad_one, grad_two = run(
            grads_kernel,
            [((2, columns, hsize), F32), ((2, part_rows, hsize), F32)],
            (grads,),
        )
    return (output, grad_one, grad_two)


def solution(mesh):
    fine = Mesh(mesh.devices.reshape(4, 4, 2, 4, 4), FEAT + NODE)
    placed = (
        P(NODE, FEAT),
        P(NODE, FEAT),
        P(NODE, None, None),
        P(NODE, None),
        P(NODE),
        P(FEAT, None),
        P(FEAT, None),
        P(),
        P(),
        P(NODE, None),
        P(NODE),
        P(NODE, None),
    )
    return jax.shard_map(
        per_device,
        mesh=fine,
        in_specs=placed,
        out_specs=(P(NODE, None), P(None, FEAT, None), P(None, FEAT, None)),
        check_vma=False,
    )
```

```python
import jax
import jax.numpy as jnp
from jax import lax
from jax.experimental import pallas as pl
from jax.experimental.pallas import tpu as pltpu
from jax.sharding import Mesh
from jax.sharding import PartitionSpec as P

BF16 = jnp.bfloat16
F32 = jnp.float32
NODE = ("x", "y")
FEAT = ("zh", "zl", "c")
NEAR = ("zl", "c")
FAN = 10
MIB = 1 << 20

VMEM = pl.BlockSpec(memory_space=pltpu.VMEM)
HBM = pl.BlockSpec(memory_space=pltpu.HBM)
ANY = pl.BlockSpec(memory_space=pl.ANY)
SMEM = pl.BlockSpec(memory_space=pltpu.SMEM)


def contract(left, right, left_dim, right_dim):
    return lax.dot_general(
        left, right, (((left_dim,), (right_dim,)), ((), ())), preferred_element_type=F32
    )


def aggregate_kernel(count_ref, index_ref, tiles_ref, feats_ref, out_ref, sources, products, total):
    slots, block, _ = tiles_ref.shape
    for position in range(sources.shape[0]):
        sources[position] = feats_ref[:, position * block : (position + 1) * block]
    out_ref[...] = jnp.zeros_like(out_ref)
    places = []
    for slot in range(slots):
        place = index_ref[0, slot]
        places.append(place)
        total[place] = jnp.zeros(total.shape[1:], F32)
    live_tiles = count_ref[...]
    for slot in range(slots):
        in_use = (slot < live_tiles).astype(F32)
        products[slot] = contract(sources[index_ref[1, slot]], tiles_ref[slot], 1, 1) * in_use
    for slot in range(slots):
        total[places[slot]] += products[slot]
    for slot in range(slots):
        out_ref[places[slot]] = total[places[slot]].astype(BF16)


def split_blocks(core, halves, mine_ref, other_ref):
    block = halves.shape[3]
    for position in range(halves.shape[0]):
        span = slice(position * block, (position + 1) * block)
        mine_ref[:, span] = halves[position, core]
        other_ref[:, span] = halves[position, 1 - core]


def owned_kernel(
    core_ref, parts_ref, targets_ref, weights_ref, blocks_ref, tmine_ref, tother_ref, mine_ref, other_ref, halves
):
    near, _, columns, block = halves.shape
    for position in range(2 * near):
        piece = targets_ref[:, position * block : (position + 1) * block]
        blocks_ref[position, :columns] = piece
        halves[position // 2, position % 2] = piece
    split_blocks(core_ref[0], halves, tmine_ref, tother_ref)
    for position in range(2 * near):
        span = slice(position * columns, (position + 1) * columns)
        total = parts_ref[0, span].astype(F32)
        for source in range(1, parts_ref.shape[0]):
            total += parts_ref[source, span].astype(F32)
        total = total.astype(BF16)
        blocks_ref[position, columns:] = total
        halves[position // 2, position % 2] = total
    split_blocks(core_ref[0], halves, mine_ref, other_ref)


def partial_kernel(blocks_ref, weights_ref, out_ref, inputs):
    group, rows, _ = blocks_ref.shape
    columns, hsize = rows // 2, out_ref.shape[1]
    depth = group * columns
    for position in range(group):
        first = position * columns
        inputs[first : first + columns] = blocks_ref[position, :columns]
        inputs[depth + first : depth + first + columns] = blocks_ref[position, columns:]
    total = contract(inputs[:depth], weights_ref[:, :hsize], 0, 0)
    total += contract(inputs[depth:], weights_ref[:, hsize:], 0, 0)
    out_ref[...] = total.astype(BF16)


def far_kernel(far_ref, own_ref, one_ref, three_ref, two_ref, picks_ref, out_ref, slots):
    far = far_ref[0]
    slots[far] = own_ref[...].astype(F32)
    for step, ref in ((2, two_ref), (1, one_ref), (3, three_ref)):
        slots[lax.rem(far + slots.shape[0] - step, slots.shape[0])] = ref[...].astype(F32)
    total = slots[0]
    for position in range(1, slots.shape[0]):
        total += slots[position]
    for position in range(out_ref.shape[0]):
        out_ref[position] = total.astype(BF16)


def picks_kernel(core_ref, neighbors_ref, seeds_ref, spread_ref, pick_ref):
    fanout, seeds = neighbors_ref.shape
    rows = spread_ref.shape[0]
    step = lax.broadcasted_iota(jnp.int32, (rows, seeds), 0)
    half = rows // 2
    first = step // half
    lane = step % 128
    side = jnp.where(first == 0, core_ref[0], 1 - core_ref[0])
    row_of = ((step % half) // 128) * 256 + side * 128 + lane
    counts = jnp.zeros((rows, seeds), F32)
    for entry in range(fanout):
        counts += (row_of == neighbors_ref[entry : entry + 1, :]).astype(F32)
    own = (row_of == seeds_ref[...]).astype(F32)
    spread_ref[:, :seeds] = counts.astype(BF16)
    spread_ref[:, seeds:] = own.astype(BF16)
    pick_ref[:seeds] = counts.T.astype(BF16)
    pick_ref[seeds:] = own.T.astype(BF16)


def activate(pre_ref, hidden_shape):
    pre_one = pre_ref[...].reshape(hidden_shape).astype(F32)
    sigmoid = jax.nn.sigmoid(pre_one)
    hidden = (pre_one * sigmoid).astype(BF16)
    return hidden, sigmoid * (1.0 + pre_one * (1.0 - sigmoid))


def mine_kernel(pre_ref, pick_ref, gathered_ref, slope_ref):
    half = slope_ref.shape[0]
    hidden, slope = activate(pre_ref, slope_ref.shape)
    gathered_ref[...] = contract(pick_ref[:, :half], hidden, 1, 0)
    slope_ref[...] = slope


def step_kernel(
    feat_ref,
    pre_ref,
    gathered_ref,
    slope_ref,
    pick_ref,
    spread_ref,
    self_ref,
    neigh_ref,
    cotangent_ref,
    targets_ref,
    targets_other_ref,
    mine_ref,
    other_ref,
    output_ref,
    grads_ref,
    gathered,
    scratch,
    output,
    output_sem,
):
    seeds = cotangent_ref.shape[0]
    columns = targets_ref.shape[0]
    half = slope_ref.shape[0]
    hidden, slope_other = activate(pre_ref, slope_ref.shape)
    gathered[...] = contract(pick_ref[:, half:], hidden, 1, 0)
    picked = gathered_ref[...] + gathered[...]
    nbr_mean = (picked[:seeds] / FAN).astype(BF16)
    own = picked[seeds:].astype(BF16)
    pre_two = contract(own, self_ref[...], 1, 0) + contract(nbr_mean, neigh_ref[...], 1, 0)
    gate = jax.nn.sigmoid(pre_two)
    output[...] = (pre_two * gate).astype(BF16)
    copy = pltpu.make_async_copy(output, output_ref, output_sem)
    copy.start()
    slope_two = (
        cotangent_ref[...].astype(F32) * (gate * (1.0 + pre_two * (1.0 - gate)))
    ).astype(BF16)

    scratch[0] = contract(own, slope_two, 0, 0)
    scratch[1] = contract(nbr_mean, slope_two, 0, 0)

    back = jnp.concatenate(
        [contract(slope_two, neigh_ref[...], 1, 1) / FAN, contract(slope_two, self_ref[...], 1, 1)],
        axis=0,
    )
    spread = spread_ref[...]
    back_hidden = contract(spread, back.astype(BF16), 1, 0)
    slope_one = jnp.concatenate(
        [
            (back_hidden[:half] * slope_ref[...]).astype(BF16),
            (back_hidden[half:] * slope_other).astype(BF16),
        ],
        axis=0,
    )
    inputs = jnp.concatenate(
        [
            jnp.concatenate([targets_ref[...], targets_other_ref[...]], axis=1),
            jnp.concatenate([mine_ref[...], other_ref[...]], axis=1),
        ],
        axis=0,
    )
    grad_one = contract(inputs, slope_one, 1, 0).astype(BF16)
    part_rows = (grads_ref.shape[1] - 2 * columns) // 2
    first = pl.multiple_of(feat_ref[0] * part_rows, part_rows)
    grad_two = jnp.concatenate(
        [scratch[0, pl.ds(first, part_rows), :], scratch[1, pl.ds(first, part_rows), :]], axis=0
    )
    every = jnp.concatenate([grad_one, grad_two.astype(BF16)], axis=0)
    for position in range(grads_ref.shape[0]):
        grads_ref[position] = every
    copy.wait()


def grads_kernel(parts_ref, one_ref, two_ref):
    total = parts_ref[0].astype(F32)
    for position in range(1, parts_ref.shape[0]):
        total += parts_ref[position].astype(F32)
    columns, part_rows = one_ref.shape[1], two_ref.shape[1]
    one_ref[0] = total[:columns]
    one_ref[1] = total[columns : 2 * columns]
    two_ref[0] = total[2 * columns : 2 * columns + part_rows]
    two_ref[1] = total[2 * columns + part_rows :]


def run(kernel, outs, operands, scratch=(), limit=8, flops=0, specs=None, out_specs=None):
    shapes = [jax.ShapeDtypeStruct(shape, dtype) for shape, dtype in outs]
    moved = sum(x.size * x.dtype.itemsize for x in operands) + sum(
        x.size * x.dtype.itemsize for x in shapes
    )
    if specs is None:
        specs = [SMEM if x.dtype == jnp.int32 and x.size == 1 else VMEM for x in operands]
    results = pl.pallas_call(
        kernel,
        out_shape=shapes,
        in_specs=specs,
        out_specs=out_specs or [VMEM] * len(shapes),
        scratch_shapes=list(scratch),
        cost_estimate=pl.CostEstimate(flops=flops, bytes_accessed=moved, transcendentals=0),
        compiler_params=pltpu.CompilerParams(vmem_limit_bytes=limit * MIB),
    )(*operands)
    return results[0] if len(shapes) == 1 else results


def per_device(
    features,
    target_feats,
    tile_values,
    tile_index,
    tile_count,
    self_weight1,
    neigh_weight1,
    self_weight2,
    neigh_weight2,
    neighbors,
    seed_index,
    cotangent,
):
    src_rows, columns = features.shape
    tgt_rows = target_feats.shape[0]
    slots, block, _ = tile_values.shape
    hsize = self_weight2.shape[0]
    seeds = seed_index.shape[0]
    owners = lax.axis_size(NODE)
    near, far = lax.axis_size("zl"), lax.axis_size("zh")
    part_rows = hsize // lax.axis_size(FEAT)
    all_blocks = tgt_rows * owners // block
    half = tgt_rows // 2
    span = half // near
    core = lax.axis_index("c").reshape(1)
    feat = lax.axis_index(FEAT).reshape(1)
    halves = pltpu.VMEM((near, 2, columns, block), BF16)
    swap = [(0, 1), (1, 0)]

    with jax.named_scope("aggregate_tiles"):
        aggregate = run(
            aggregate_kernel,
            [((all_blocks, columns, block), BF16)],
            (tile_count.reshape(1, 1), tile_index.T, tile_values, features.T),
            [
                pltpu.VMEM((src_rows // block, columns, block), BF16),
                pltpu.VMEM((slots, columns, block), F32),
                pltpu.VMEM((all_blocks, columns, block), F32),
            ],
            limit=56,
            specs=[VMEM, SMEM, VMEM, VMEM],
        )
    with jax.named_scope("aggregate_exchange"):
        parts = lax.all_to_all(
            aggregate.reshape(owners, tgt_rows // block * columns, block), NODE, 0, 0, tiled=True
        )
    with jax.named_scope("weights_gather"):
        weights = jnp.concatenate([self_weight1, neigh_weight1], axis=1)
        weights = lax.all_gather(weights, NEAR, tiled=True)
    with jax.named_scope("owned_sum"):
        blocks, targets_mine, targets_other, agg_mine, agg_other = run(
            owned_kernel,
            [((2 * near, 2 * columns, block), BF16)] + [((columns, half), BF16)] * 4,
            (core, parts, target_feats.T, weights),
            [halves],
            specs=[SMEM, VMEM, VMEM, ANY],
        )
    with jax.named_scope("near_exchange"):
        blocks = lax.all_to_all(blocks, NEAR, 0, 0, tiled=True)
    with jax.named_scope("partial_pre"):
        quarter = run(
            partial_kernel,
            [((span, hsize), BF16)],
            (blocks, weights),
            [pltpu.VMEM((4 * near * columns, span), BF16)],
        )
    with jax.named_scope("picks"):
        spread, pick = run(
            picks_kernel,
            [((tgt_rows, 2 * seeds), BF16), ((2 * seeds, tgt_rows), BF16)],
            (core, neighbors.T, seed_index.reshape(1, -1)),
            limit=16,
            flops=20 * tgt_rows * seeds,
        )
    with jax.named_scope("pre_sum_far"):
        arrived = [
            lax.ppermute(quarter, "zh", [(i, (i + step) % far) for i in range(far)])
            for step in (1, 3, 2)
        ]
        copies = run(
            far_kernel,
            [((near, span, hsize), BF16)],
            (lax.axis_index("zh").reshape(1), quarter, *arrived, pick),
            [pltpu.VMEM((far, span, hsize), F32)],
            specs=[SMEM] + [VMEM] * 4 + [ANY],
        )
    with jax.named_scope("pre_gather"):
        pre_mine = lax.all_to_all(copies, "zl", 0, 0, tiled=True)
        pre_other = lax.ppermute(pre_mine, "c", swap)
    with jax.named_scope("step_mine"):
        gathered, slope = run(
            mine_kernel,
            [((2 * seeds, hsize), F32), ((half, hsize), F32)],
            (pre_mine, pick),
            limit=12,
            flops=4 * seeds * half * hsize,
        )
    with jax.named_scope("step"):
        output, grads = run(
            step_kernel,
            [(cotangent.shape, BF16), ((owners, 2 * columns + 2 * part_rows, hsize), BF16)],
            (
                feat,
                pre_other,
                gathered,
                slope,
                pick,
                spread,
                self_weight2,
                neigh_weight2,
                cotangent,
                targets_mine,
                targets_other,
                agg_mine,
                agg_other,
            ),
            [
                pltpu.VMEM((2 * seeds, hsize), F32),
                pltpu.VMEM((2, hsize, hsize), F32),
                pltpu.VMEM(cotangent.shape, BF16),
                pltpu.SemaphoreType.DMA,
            ],
            limit=24,
            out_specs=[HBM, VMEM],
        )
    with jax.named_scope("grad_sum"):
        grads = lax.all_to_all(grads, NODE, 0, 0, tiled=True)
        grad_one, grad_two = run(
            grads_kernel,
            [((2, columns, hsize), F32), ((2, part_rows, hsize), F32)],
            (grads,),
        )
    return (output, grad_one, grad_two)


def solution(mesh):
    fine = Mesh(mesh.devices.reshape(4, 4, 2, 4, 4), FEAT + NODE)
    placed = (
        P(NODE, FEAT),
        P(NODE, FEAT),
        P(NODE, None, None),
        P(NODE, None),
        P(NODE),
        P(FEAT, None),
        P(FEAT, None),
        P(),
        P(),
        P(NODE, None),
        P(NODE),
        P(NODE, None),
    )
    return jax.shard_map(
        per_device,
        mesh=fine,
        in_specs=placed,
        out_specs=(P(NODE, None), P(None, FEAT, None), P(None, FEAT, None)),
        check_vma=False,
    )
```

```python
import jax
import jax.numpy as jnp
from jax import lax
from jax.experimental import pallas as pl
from jax.experimental.pallas import tpu as pltpu
from jax.sharding import Mesh
from jax.sharding import PartitionSpec as P

BF16 = jnp.bfloat16
F32 = jnp.float32
NODE = ("x", "y")
FEAT = ("zh", "zl", "c")
NEAR = ("zl", "c")
FAN = 10
MIB = 1 << 20

VMEM = pl.BlockSpec(memory_space=pltpu.VMEM)
HBM = pl.BlockSpec(memory_space=pltpu.HBM)
ANY = pl.BlockSpec(memory_space=pl.ANY)
SMEM = pl.BlockSpec(memory_space=pltpu.SMEM)


def contract(left, right, left_dim, right_dim):
    return lax.dot_general(
        left, right, (((left_dim,), (right_dim,)), ((), ())), preferred_element_type=F32
    )


def aggregate_kernel(count_ref, index_ref, tiles_ref, feats_ref, out_ref, sources, products, total):
    slots, block, _ = tiles_ref.shape
    for position in range(sources.shape[0]):
        sources[position] = feats_ref[:, position * block : (position + 1) * block]
    out_ref[...] = jnp.zeros_like(out_ref)
    places = []
    for slot in range(slots):
        place = index_ref[0, slot]
        places.append(place)
        total[place] = jnp.zeros(total.shape[1:], F32)
    live_tiles = count_ref[...]
    for slot in range(slots):
        in_use = (slot < live_tiles).astype(F32)
        products[slot] = contract(sources[index_ref[1, slot]], tiles_ref[slot], 1, 1) * in_use
    for slot in range(slots):
        total[places[slot]] += products[slot]
    for slot in range(slots):
        out_ref[places[slot]] = total[places[slot]].astype(BF16)


def split_blocks(core, halves, mine_ref, other_ref):
    block = halves.shape[3]
    for position in range(halves.shape[0]):
        span = slice(position * block, (position + 1) * block)
        mine_ref[:, span] = halves[position, core]
        other_ref[:, span] = halves[position, 1 - core]


def owned_kernel(
    core_ref, parts_ref, targets_ref, weights_ref, blocks_ref, tmine_ref, tother_ref, mine_ref, other_ref, halves
):
    near, _, columns, block = halves.shape
    for position in range(2 * near):
        piece = targets_ref[:, position * block : (position + 1) * block]
        blocks_ref[position, :columns] = piece
        halves[position // 2, position % 2] = piece
    split_blocks(core_ref[0], halves, tmine_ref, tother_ref)
    for position in range(2 * near):
        span = slice(position * columns, (position + 1) * columns)
        total = parts_ref[0, span].astype(F32)
        for source in range(1, parts_ref.shape[0]):
            total += parts_ref[source, span].astype(F32)
        total = total.astype(BF16)
        blocks_ref[position, columns:] = total
        halves[position // 2, position % 2] = total
    split_blocks(core_ref[0], halves, mine_ref, other_ref)


def partial_kernel(blocks_ref, weights_ref, out_ref, inputs):
    group, rows, _ = blocks_ref.shape
    columns, hsize = rows // 2, out_ref.shape[1]
    depth = group * columns
    for position in range(group):
        first = position * columns
        inputs[first : first + columns] = blocks_ref[position, :columns]
        inputs[depth + first : depth + first + columns] = blocks_ref[position, columns:]
    total = contract(inputs[:depth], weights_ref[:, :hsize], 0, 0)
    total += contract(inputs[depth:], weights_ref[:, hsize:], 0, 0)
    out_ref[...] = total.astype(BF16)


def far_kernel(parts_ref, picks_ref, out_ref):
    total = parts_ref[0].astype(F32)
    for position in range(1, parts_ref.shape[0]):
        total += parts_ref[position].astype(F32)
    total = total.astype(BF16)
    for position in range(out_ref.shape[0]):
        out_ref[position] = total


def picks_kernel(core_ref, neighbors_ref, seeds_ref, spread_ref, pick_ref):
    fanout, seeds = neighbors_ref.shape
    rows = spread_ref.shape[0]
    step = lax.broadcasted_iota(jnp.int32, (rows, seeds), 0)
    half = rows // 2
    first = step // half
    lane = step % 128
    side = jnp.where(first == 0, core_ref[0], 1 - core_ref[0])
    row_of = ((step % half) // 128) * 256 + side * 128 + lane
    counts = jnp.zeros((rows, seeds), F32)
    for entry in range(fanout):
        counts += (row_of == neighbors_ref[entry : entry + 1, :]).astype(F32)
    own = (row_of == seeds_ref[...]).astype(F32)
    spread_ref[:, :seeds] = counts.astype(BF16)
    spread_ref[:, seeds:] = own.astype(BF16)
    pick_ref[:seeds] = counts.T.astype(BF16)
    pick_ref[seeds:] = own.T.astype(BF16)


def activate(pre_ref, hidden_shape):
    pre_one = pre_ref[...].reshape(hidden_shape).astype(F32)
    sigmoid = jax.nn.sigmoid(pre_one)
    hidden = (pre_one * sigmoid).astype(BF16)
    return hidden, sigmoid * (1.0 + pre_one * (1.0 - sigmoid))


def mine_kernel(pre_ref, pick_ref, gathered_ref, slope_ref):
    half = slope_ref.shape[0]
    hidden, slope = activate(pre_ref, slope_ref.shape)
    gathered_ref[...] = contract(pick_ref[:, :half], hidden, 1, 0)
    slope_ref[...] = slope


def step_kernel(
    feat_ref,
    pre_ref,
    gathered_ref,
    slope_ref,
    pick_ref,
    spread_ref,
    self_ref,
    neigh_ref,
    cotangent_ref,
    targets_ref,
    targets_other_ref,
    mine_ref,
    other_ref,
    output_ref,
    grads_ref,
    gathered,
    scratch,
    output,
    output_sem,
):
    seeds = cotangent_ref.shape[0]
    columns = targets_ref.shape[0]
    half = slope_ref.shape[0]
    hidden, slope_other = activate(pre_ref, slope_ref.shape)
    gathered[...] = contract(pick_ref[:, half:], hidden, 1, 0)
    picked = gathered_ref[...] + gathered[...]
    nbr_mean = (picked[:seeds] / FAN).astype(BF16)
    own = picked[seeds:].astype(BF16)
    pre_two = contract(own, self_ref[...], 1, 0) + contract(nbr_mean, neigh_ref[...], 1, 0)
    gate = jax.nn.sigmoid(pre_two)
    output[...] = (pre_two * gate).astype(BF16)
    copy = pltpu.make_async_copy(output, output_ref, output_sem)
    copy.start()
    slope_two = (
        cotangent_ref[...].astype(F32) * (gate * (1.0 + pre_two * (1.0 - gate)))
    ).astype(BF16)

    scratch[0] = contract(own, slope_two, 0, 0)
    scratch[1] = contract(nbr_mean, slope_two, 0, 0)

    back = jnp.concatenate(
        [contract(slope_two, neigh_ref[...], 1, 1) / FAN, contract(slope_two, self_ref[...], 1, 1)],
        axis=0,
    )
    spread = spread_ref[...]
    back_hidden = contract(spread, back.astype(BF16), 1, 0)
    slope_one = jnp.concatenate(
        [
            (back_hidden[:half] * slope_ref[...]).astype(BF16),
            (back_hidden[half:] * slope_other).astype(BF16),
        ],
        axis=0,
    )
    inputs = jnp.concatenate(
        [
            jnp.concatenate([targets_ref[...], targets_other_ref[...]], axis=1),
            jnp.concatenate([mine_ref[...], other_ref[...]], axis=1),
        ],
        axis=0,
    )
    grad_one = contract(inputs, slope_one, 1, 0).astype(BF16)
    part_rows = (grads_ref.shape[1] - 2 * columns) // 2
    first = pl.multiple_of(feat_ref[0] * part_rows, part_rows)
    grad_two = jnp.concatenate(
        [scratch[0, pl.ds(first, part_rows), :], scratch[1, pl.ds(first, part_rows), :]], axis=0
    )
    every = jnp.concatenate([grad_one, grad_two.astype(BF16)], axis=0)
    for position in range(grads_ref.shape[0]):
        grads_ref[position] = every
    copy.wait()


def grads_kernel(parts_ref, one_ref, two_ref):
    total = parts_ref[0].astype(F32)
    for position in range(1, parts_ref.shape[0]):
        total += parts_ref[position].astype(F32)
    columns, part_rows = one_ref.shape[1], two_ref.shape[1]
    one_ref[0] = total[:columns]
    one_ref[1] = total[columns : 2 * columns]
    two_ref[0] = total[2 * columns : 2 * columns + part_rows]
    two_ref[1] = total[2 * columns + part_rows :]


def run(kernel, outs, operands, scratch=(), limit=8, flops=0, specs=None, out_specs=None):
    shapes = [jax.ShapeDtypeStruct(shape, dtype) for shape, dtype in outs]
    moved = sum(x.size * x.dtype.itemsize for x in operands) + sum(
        x.size * x.dtype.itemsize for x in shapes
    )
    if specs is None:
        specs = [SMEM if x.dtype == jnp.int32 and x.size == 1 else VMEM for x in operands]
    results = pl.pallas_call(
        kernel,
        out_shape=shapes,
        in_specs=specs,
        out_specs=out_specs or [VMEM] * len(shapes),
        scratch_shapes=list(scratch),
        cost_estimate=pl.CostEstimate(flops=flops, bytes_accessed=moved, transcendentals=0),
        compiler_params=pltpu.CompilerParams(vmem_limit_bytes=limit * MIB),
    )(*operands)
    return results[0] if len(shapes) == 1 else results


def per_device(
    features,
    target_feats,
    tile_values,
    tile_index,
    tile_count,
    self_weight1,
    neigh_weight1,
    self_weight2,
    neigh_weight2,
    neighbors,
    seed_index,
    cotangent,
):
    src_rows, columns = features.shape
    tgt_rows = target_feats.shape[0]
    slots, block, _ = tile_values.shape
    hsize = self_weight2.shape[0]
    seeds = seed_index.shape[0]
    owners = lax.axis_size(NODE)
    near, far = lax.axis_size("zl"), lax.axis_size("zh")
    part_rows = hsize // lax.axis_size(FEAT)
    all_blocks = tgt_rows * owners // block
    half = tgt_rows // 2
    span = half // near
    core = lax.axis_index("c").reshape(1)
    feat = lax.axis_index(FEAT).reshape(1)
    halves = pltpu.VMEM((near, 2, columns, block), BF16)
    swap = [(0, 1), (1, 0)]

    with jax.named_scope("aggregate_tiles"):
        aggregate = run(
            aggregate_kernel,
            [((all_blocks, columns, block), BF16)],
            (tile_count.reshape(1, 1), tile_index.T, tile_values, features.T),
            [
                pltpu.VMEM((src_rows // block, columns, block), BF16),
                pltpu.VMEM((slots, columns, block), F32),
                pltpu.VMEM((all_blocks, columns, block), F32),
            ],
            limit=56,
            specs=[VMEM, SMEM, VMEM, VMEM],
        )
    with jax.named_scope("aggregate_exchange"):
        parts = lax.all_to_all(
            aggregate.reshape(owners, tgt_rows // block * columns, block), NODE, 0, 0, tiled=True
        )
    with jax.named_scope("weights_gather"):
        weights = jnp.concatenate([self_weight1, neigh_weight1], axis=1)
        weights = lax.all_gather(weights, NEAR, tiled=True)
    with jax.named_scope("owned_sum"):
        blocks, targets_mine, targets_other, agg_mine, agg_other = run(
            owned_kernel,
            [((2 * near, 2 * columns, block), BF16)] + [((columns, half), BF16)] * 4,
            (core, parts, target_feats.T, weights),
            [halves],
            specs=[SMEM, VMEM, VMEM, ANY],
        )
    with jax.named_scope("near_exchange"):
        blocks = lax.all_to_all(blocks, NEAR, 0, 0, tiled=True)
    with jax.named_scope("partial_pre"):
        quarter = run(
            partial_kernel,
            [((span, hsize), BF16)],
            (blocks, weights),
            [pltpu.VMEM((4 * near * columns, span), BF16)],
        )
    with jax.named_scope("picks"):
        spread, pick = run(
            picks_kernel,
            [((tgt_rows, 2 * seeds), BF16), ((2 * seeds, tgt_rows), BF16)],
            (core, neighbors.T, seed_index.reshape(1, -1)),
            limit=16,
            flops=20 * tgt_rows * seeds,
        )
    with jax.named_scope("pre_sum_far"):
        parts = lax.all_gather(quarter, "zh")
        copies = run(
            far_kernel,
            [((near, span, hsize), BF16)],
            (parts, pick),
            specs=[VMEM, ANY],
        )
    with jax.named_scope("pre_gather"):
        pre_mine = lax.all_to_all(copies, "zl", 0, 0, tiled=True)
        pre_other = lax.ppermute(pre_mine, "c", swap)
    with jax.named_scope("step_mine"):
        gathered, slope = run(
            mine_kernel,
            [((2 * seeds, hsize), F32), ((half, hsize), F32)],
            (pre_mine, pick),
            limit=12,
            flops=4 * seeds * half * hsize,
        )
    with jax.named_scope("step"):
        output, grads = run(
            step_kernel,
            [(cotangent.shape, BF16), ((owners, 2 * columns + 2 * part_rows, hsize), BF16)],
            (
                feat,
                pre_other,
                gathered,
                slope,
                pick,
                spread,
                self_weight2,
                neigh_weight2,
                cotangent,
                targets_mine,
                targets_other,
                agg_mine,
                agg_other,
            ),
            [
                pltpu.VMEM((2 * seeds, hsize), F32),
                pltpu.VMEM((2, hsize, hsize), F32),
                pltpu.VMEM(cotangent.shape, BF16),
                pltpu.SemaphoreType.DMA,
            ],
            limit=24,
            out_specs=[HBM, VMEM],
        )
    with jax.named_scope("grad_sum"):
        grads = lax.all_to_all(grads, NODE, 0, 0, tiled=True)
        grad_one, grad_two = run(
            grads_kernel,
            [((2, columns, hsize), F32), ((2, part_rows, hsize), F32)],
            (grads,),
        )
    return (output, grad_one, grad_two)


def solution(mesh):
    fine = Mesh(mesh.devices.reshape(4, 4, 2, 4, 4), FEAT + NODE)
    placed = (
        P(NODE, FEAT),
        P(NODE, FEAT),
        P(NODE, None, None),
        P(NODE, None),
        P(NODE),
        P(FEAT, None),
        P(FEAT, None),
        P(),
        P(),
        P(NODE, None),
        P(NODE),
        P(NODE, None),
    )
    return jax.shard_map(
        per_device,
        mesh=fine,
        in_specs=placed,
        out_specs=(P(NODE, None), P(None, FEAT, None), P(None, FEAT, None)),
        check_vma=False,
    )
```

```python
import jax
import jax.numpy as jnp
from jax import lax
from jax.experimental import pallas as pl
from jax.experimental.pallas import tpu as pltpu
from jax.sharding import Mesh
from jax.sharding import PartitionSpec as P

BF16 = jnp.bfloat16
F32 = jnp.float32
NODE = ("x", "y")
FEAT = ("zh", "zl", "c")
NEAR = ("zl", "c")
FAN = 10
MIB = 1 << 20

VMEM = pl.BlockSpec(memory_space=pltpu.VMEM)
ANY = pl.BlockSpec(memory_space=pl.ANY)
SMEM = pl.BlockSpec(memory_space=pltpu.SMEM)


def contract(left, right, left_dim, right_dim):
    return lax.dot_general(
        left, right, (((left_dim,), (right_dim,)), ((), ())), preferred_element_type=F32
    )


def aggregate_kernel(count_ref, index_ref, tiles_ref, feats_ref, out_ref, sources, products, total):
    slots, block, _ = tiles_ref.shape
    for position in range(sources.shape[0]):
        sources[position] = feats_ref[:, position * block : (position + 1) * block]
    out_ref[...] = jnp.zeros_like(out_ref)
    places = []
    for slot in range(slots):
        place = index_ref[0, slot]
        places.append(place)
        total[place] = jnp.zeros(total.shape[1:], F32)
    live_tiles = count_ref[...]
    for slot in range(slots):
        in_use = (slot < live_tiles).astype(F32)
        products[slot] = contract(sources[index_ref[1, slot]], tiles_ref[slot], 1, 1) * in_use
    for slot in range(slots):
        total[places[slot]] += products[slot]
    for slot in range(slots):
        out_ref[places[slot]] = total[places[slot]].astype(BF16)


def split_blocks(core, halves, mine_ref, other_ref):
    block = halves.shape[3]
    for position in range(halves.shape[0]):
        span = slice(position * block, (position + 1) * block)
        mine_ref[:, span] = halves[position, core]
        other_ref[:, span] = halves[position, 1 - core]


def owned_kernel(
    core_ref, parts_ref, targets_ref, weights_ref, blocks_ref, tmine_ref, tother_ref, mine_ref, other_ref, halves
):
    near, _, columns, block = halves.shape
    for position in range(2 * near):
        piece = targets_ref[:, position * block : (position + 1) * block]
        blocks_ref[position, :columns] = piece
        halves[position // 2, position % 2] = piece
    split_blocks(core_ref[0], halves, tmine_ref, tother_ref)
    for position in range(2 * near):
        span = slice(position * columns, (position + 1) * columns)
        total = parts_ref[0, span].astype(F32)
        for source in range(1, parts_ref.shape[0]):
            total += parts_ref[source, span].astype(F32)
        total = total.astype(BF16)
        blocks_ref[position, columns:] = total
        halves[position // 2, position % 2] = total
    split_blocks(core_ref[0], halves, mine_ref, other_ref)


def partial_kernel(blocks_ref, weights_ref, out_ref, inputs):
    group, rows, _ = blocks_ref.shape
    columns, hsize = rows // 2, out_ref.shape[1]
    depth = group * columns
    for position in range(group):
        first = position * columns
        inputs[first : first + columns] = blocks_ref[position, :columns]
        inputs[depth + first : depth + first + columns] = blocks_ref[position, columns:]
    total = contract(inputs[:depth], weights_ref[:, :hsize], 0, 0)
    total += contract(inputs[depth:], weights_ref[:, hsize:], 0, 0)
    out_ref[...] = total.astype(BF16)


def far_kernel(parts_ref, picks_ref, out_ref):
    total = parts_ref[0].astype(F32)
    for position in range(1, parts_ref.shape[0]):
        total += parts_ref[position].astype(F32)
    total = total.astype(BF16)
    for position in range(out_ref.shape[0]):
        out_ref[position] = total


def picks_kernel(core_ref, neighbors_ref, seeds_ref, spread_ref, pick_ref):
    fanout, seeds = neighbors_ref.shape
    rows = spread_ref.shape[0]
    step = lax.broadcasted_iota(jnp.int32, (rows, seeds), 0)
    half = rows // 2
    first = step // half
    lane = step % 128
    side = jnp.where(first == 0, core_ref[0], 1 - core_ref[0])
    row_of = ((step % half) // 128) * 256 + side * 128 + lane
    counts = jnp.zeros((rows, seeds), F32)
    for entry in range(fanout):
        counts += (row_of == neighbors_ref[entry : entry + 1, :]).astype(F32)
    own = (row_of == seeds_ref[...]).astype(F32)
    spread_ref[:, :seeds] = counts.astype(BF16)
    spread_ref[:, seeds:] = own.astype(BF16)
    pick_ref[:seeds] = counts.T.astype(BF16)
    pick_ref[seeds:] = own.T.astype(BF16)


def activate(pre_ref, hidden_shape):
    pre_one = pre_ref[...].reshape(hidden_shape).astype(F32)
    sigmoid = jax.nn.sigmoid(pre_one)
    hidden = (pre_one * sigmoid).astype(BF16)
    return hidden, sigmoid * (1.0 + pre_one * (1.0 - sigmoid))


def mine_kernel(pre_ref, pick_ref, gathered_ref, slope_ref):
    half = slope_ref.shape[0]
    hidden, slope = activate(pre_ref, slope_ref.shape)
    gathered_ref[...] = contract(pick_ref[:, :half], hidden, 1, 0)
    slope_ref[...] = slope


def step_kernel(
    feat_ref,
    pre_ref,
    gathered_ref,
    slope_ref,
    pick_ref,
    spread_ref,
    self_ref,
    neigh_ref,
    cotangent_ref,
    targets_ref,
    targets_other_ref,
    mine_ref,
    other_ref,
    output_ref,
    grads_ref,
    gathered,
    scratch,
):
    seeds = cotangent_ref.shape[0]
    columns = targets_ref.shape[0]
    half = slope_ref.shape[0]
    hidden, slope_other = activate(pre_ref, slope_ref.shape)
    gathered[...] = contract(pick_ref[:, half:], hidden, 1, 0)
    picked = gathered_ref[...] + gathered[...]
    nbr_mean = (picked[:seeds] / FAN).astype(BF16)
    own = picked[seeds:].astype(BF16)
    pre_two = contract(own, self_ref[...], 1, 0) + contract(nbr_mean, neigh_ref[...], 1, 0)
    gate = jax.nn.sigmoid(pre_two)
    output_ref[...] = (pre_two * gate).astype(BF16)
    slope_two = (
        cotangent_ref[...].astype(F32) * (gate * (1.0 + pre_two * (1.0 - gate)))
    ).astype(BF16)

    scratch[0] = contract(own, slope_two, 0, 0)
    scratch[1] = contract(nbr_mean, slope_two, 0, 0)

    back = jnp.concatenate(
        [contract(slope_two, neigh_ref[...], 1, 1) / FAN, contract(slope_two, self_ref[...], 1, 1)],
        axis=0,
    )
    spread = spread_ref[...]
    back_hidden = contract(spread, back.astype(BF16), 1, 0)
    slope_one = jnp.concatenate(
        [
            (back_hidden[:half] * slope_ref[...]).astype(BF16),
            (back_hidden[half:] * slope_other).astype(BF16),
        ],
        axis=0,
    )
    inputs = jnp.concatenate(
        [
            jnp.concatenate([targets_ref[...], targets_other_ref[...]], axis=1),
            jnp.concatenate([mine_ref[...], other_ref[...]], axis=1),
        ],
        axis=0,
    )
    grad_one = contract(inputs, slope_one, 1, 0).astype(BF16)
    part_rows = (grads_ref.shape[1] - 2 * columns) // 2
    first = pl.multiple_of(feat_ref[0] * part_rows, part_rows)
    grad_two = jnp.concatenate(
        [scratch[0, pl.ds(first, part_rows), :], scratch[1, pl.ds(first, part_rows), :]], axis=0
    )
    every = jnp.concatenate([grad_one, grad_two.astype(BF16)], axis=0)
    for position in range(grads_ref.shape[0]):
        grads_ref[position] = every


def grads_kernel(parts_ref, output_ref, one_ref, two_ref, final_ref):
    final_ref[...] = output_ref[...]
    total = parts_ref[0].astype(F32)
    for position in range(1, parts_ref.shape[0]):
        total += parts_ref[position].astype(F32)
    columns, part_rows = one_ref.shape[1], two_ref.shape[1]
    one_ref[0] = total[:columns]
    one_ref[1] = total[columns : 2 * columns]
    two_ref[0] = total[2 * columns : 2 * columns + part_rows]
    two_ref[1] = total[2 * columns + part_rows :]


def run(kernel, outs, operands, scratch=(), limit=8, flops=0, specs=None):
    shapes = [jax.ShapeDtypeStruct(shape, dtype) for shape, dtype in outs]
    moved = sum(x.size * x.dtype.itemsize for x in operands) + sum(
        x.size * x.dtype.itemsize for x in shapes
    )
    if specs is None:
        specs = [SMEM if x.dtype == jnp.int32 and x.size == 1 else VMEM for x in operands]
    results = pl.pallas_call(
        kernel,
        out_shape=shapes,
        in_specs=specs,
        out_specs=[VMEM] * len(shapes),
        scratch_shapes=list(scratch),
        cost_estimate=pl.CostEstimate(flops=flops, bytes_accessed=moved, transcendentals=0),
        compiler_params=pltpu.CompilerParams(vmem_limit_bytes=limit * MIB),
    )(*operands)
    return results[0] if len(shapes) == 1 else results


def per_device(
    features,
    target_feats,
    tile_values,
    tile_index,
    tile_count,
    self_weight1,
    neigh_weight1,
    self_weight2,
    neigh_weight2,
    neighbors,
    seed_index,
    cotangent,
):
    src_rows, columns = features.shape
    tgt_rows = target_feats.shape[0]
    slots, block, _ = tile_values.shape
    hsize = self_weight2.shape[0]
    seeds = seed_index.shape[0]
    owners = lax.axis_size(NODE)
    near, far = lax.axis_size("zl"), lax.axis_size("zh")
    part_rows = hsize // lax.axis_size(FEAT)
    all_blocks = tgt_rows * owners // block
    half = tgt_rows // 2
    span = half // near
    core = lax.axis_index("c").reshape(1)
    feat = lax.axis_index(FEAT).reshape(1)
    halves = pltpu.VMEM((near, 2, columns, block), BF16)
    swap = [(0, 1), (1, 0)]

    with jax.named_scope("aggregate_tiles"):
        aggregate = run(
            aggregate_kernel,
            [((all_blocks, columns, block), BF16)],
            (tile_count.reshape(1, 1), tile_index.T, tile_values, features.T),
            [
                pltpu.VMEM((src_rows // block, columns, block), BF16),
                pltpu.VMEM((slots, columns, block), F32),
                pltpu.VMEM((all_blocks, columns, block), F32),
            ],
            limit=56,
            specs=[VMEM, SMEM, VMEM, VMEM],
        )
    with jax.named_scope("aggregate_exchange"):
        parts = lax.all_to_all(
            aggregate.reshape(owners, tgt_rows // block * columns, block), NODE, 0, 0, tiled=True
        )
    with jax.named_scope("weights_gather"):
        weights = jnp.concatenate([self_weight1, neigh_weight1], axis=1)
        weights = lax.all_gather(weights, NEAR, tiled=True)
    with jax.named_scope("owned_sum"):
        blocks, targets_mine, targets_other, agg_mine, agg_other = run(
            owned_kernel,
            [((2 * near, 2 * columns, block), BF16)] + [((columns, half), BF16)] * 4,
            (core, parts, target_feats.T, weights),
            [halves],
            specs=[SMEM, VMEM, VMEM, ANY],
        )
    with jax.named_scope("near_exchange"):
        blocks = lax.all_to_all(blocks, NEAR, 0, 0, tiled=True)
    with jax.named_scope("partial_pre"):
        quarter = run(
            partial_kernel,
            [((span, hsize), BF16)],
            (blocks, weights),
            [pltpu.VMEM((4 * near * columns, span), BF16)],
        )
    with jax.named_scope("picks"):
        spread, pick = run(
            picks_kernel,
            [((tgt_rows, 2 * seeds), BF16), ((2 * seeds, tgt_rows), BF16)],
            (core, neighbors.T, seed_index.reshape(1, -1)),
            limit=16,
            flops=20 * tgt_rows * seeds,
        )
    with jax.named_scope("pre_sum_far"):
        parts = lax.all_gather(quarter, "zh")
        copies = run(
            far_kernel,
            [((near, span, hsize), BF16)],
            (parts, pick),
            specs=[VMEM, ANY],
        )
    with jax.named_scope("pre_gather"):
        pre_mine = lax.all_to_all(copies, "zl", 0, 0, tiled=True)
        pre_other = lax.ppermute(pre_mine, "c", swap)
    with jax.named_scope("step_mine"):
        gathered, slope = run(
            mine_kernel,
            [((2 * seeds, hsize), F32), ((half, hsize), F32)],
            (pre_mine, pick),
            limit=12,
            flops=4 * seeds * half * hsize,
        )
    with jax.named_scope("step"):
        output, grads = run(
            step_kernel,
            [(cotangent.shape, BF16), ((owners, 2 * columns + 2 * part_rows, hsize), BF16)],
            (
                feat,
                pre_other,
                gathered,
                slope,
                pick,
                spread,
                self_weight2,
                neigh_weight2,
                cotangent,
                targets_mine,
                targets_other,
                agg_mine,
                agg_other,
            ),
            [
                pltpu.VMEM((2 * seeds, hsize), F32),
                pltpu.VMEM((2, hsize, hsize), F32),
            ],
            limit=24,
        )
    with jax.named_scope("grad_sum"):
        grads = lax.all_to_all(grads, NODE, 0, 0, tiled=True)
        grad_one, grad_two, output = run(
            grads_kernel,
            [((2, columns, hsize), F32), ((2, part_rows, hsize), F32), (cotangent.shape, BF16)],
            (grads, output),
        )
    return (output, grad_one, grad_two)


def solution(mesh):
    fine = Mesh(mesh.devices.reshape(4, 4, 2, 4, 4), FEAT + NODE)
    placed = (
        P(NODE, FEAT),
        P(NODE, FEAT),
        P(NODE, None, None),
        P(NODE, None),
        P(NODE),
        P(FEAT, None),
        P(FEAT, None),
        P(),
        P(),
        P(NODE, None),
        P(NODE),
        P(NODE, None),
    )
    return jax.shard_map(
        per_device,
        mesh=fine,
        in_specs=placed,
        out_specs=(P(NODE, None), P(None, FEAT, None), P(None, FEAT, None)),
        check_vma=False,
    )
```

```python
import jax
import jax.numpy as jnp
from jax import lax
from jax.experimental import pallas as pl
from jax.experimental.pallas import tpu as pltpu
from jax.sharding import Mesh
from jax.sharding import PartitionSpec as P

BF16 = jnp.bfloat16
F32 = jnp.float32
NODE = ("x", "y")
FEAT = ("zh", "zl", "c")
NEAR = ("zl", "c")
FAN = 10
MIB = 1 << 20

VMEM = pl.BlockSpec(memory_space=pltpu.VMEM)
ANY = pl.BlockSpec(memory_space=pl.ANY)
SMEM = pl.BlockSpec(memory_space=pltpu.SMEM)


def contract(left, right, left_dim, right_dim):
    return lax.dot_general(
        left, right, (((left_dim,), (right_dim,)), ((), ())), preferred_element_type=F32
    )


def aggregate_kernel(count_ref, index_ref, tiles_ref, feats_ref, out_ref, sources, products, total):
    slots, block, _ = tiles_ref.shape
    for position in range(sources.shape[0]):
        sources[position] = feats_ref[:, position * block : (position + 1) * block]
    out_ref[...] = jnp.zeros_like(out_ref)
    places = []
    for slot in range(slots):
        place = index_ref[0, slot]
        places.append(place)
        total[place] = jnp.zeros(total.shape[1:], F32)
    live_tiles = count_ref[...]
    for slot in range(slots):
        in_use = (slot < live_tiles).astype(F32)
        products[slot] = contract(sources[index_ref[1, slot]], tiles_ref[slot], 1, 1) * in_use
    for slot in range(slots):
        total[places[slot]] += products[slot]
    for slot in range(slots):
        out_ref[places[slot]] = total[places[slot]].astype(BF16)


def split_blocks(core, halves, mine_ref, other_ref):
    block = halves.shape[3]
    for position in range(halves.shape[0]):
        span = slice(position * block, (position + 1) * block)
        mine_ref[:, span] = halves[position, core]
        other_ref[:, span] = halves[position, 1 - core]


def owned_kernel(
    core_ref, parts_ref, targets_ref, weights_ref, blocks_ref, tmine_ref, tother_ref, mine_ref, other_ref, halves
):
    near, _, columns, block = halves.shape
    for position in range(2 * near):
        piece = targets_ref[:, position * block : (position + 1) * block]
        blocks_ref[position, :columns] = piece
        halves[position // 2, position % 2] = piece
    split_blocks(core_ref[0], halves, tmine_ref, tother_ref)
    for position in range(2 * near):
        span = slice(position * columns, (position + 1) * columns)
        total = parts_ref[0, span].astype(F32)
        for source in range(1, parts_ref.shape[0]):
            total += parts_ref[source, span].astype(F32)
        total = total.astype(BF16)
        blocks_ref[position, columns:] = total
        halves[position // 2, position % 2] = total
    split_blocks(core_ref[0], halves, mine_ref, other_ref)


def partial_kernel(blocks_ref, weights_ref, out_ref, inputs):
    group, rows, _ = blocks_ref.shape
    columns, hsize = rows // 2, out_ref.shape[1]
    depth = group * columns
    for position in range(group):
        first = position * columns
        inputs[first : first + columns] = blocks_ref[position, :columns]
        inputs[depth + first : depth + first + columns] = blocks_ref[position, columns:]
    total = contract(inputs[:depth], weights_ref[:, :hsize], 0, 0)
    total += contract(inputs[depth:], weights_ref[:, hsize:], 0, 0)
    out_ref[...] = total.astype(BF16)


def far_kernel(parts_ref, picks_ref, out_ref):
    total = parts_ref[0].astype(F32)
    for position in range(1, parts_ref.shape[0]):
        total += parts_ref[position].astype(F32)
    total = total.astype(BF16)
    for position in range(out_ref.shape[0]):
        out_ref[position] = total


def picks_kernel(core_ref, neighbors_ref, seeds_ref, spread_ref, pick_ref):
    fanout, seeds = neighbors_ref.shape
    rows = spread_ref.shape[0]
    step = lax.broadcasted_iota(jnp.int32, (rows, seeds), 0)
    half = rows // 2
    first = step // half
    lane = step % 128
    side = jnp.where(first == 0, core_ref[0], 1 - core_ref[0])
    row_of = ((step % half) // 128) * 256 + side * 128 + lane
    counts = jnp.zeros((rows, seeds), F32)
    for entry in range(fanout):
        counts += (row_of == neighbors_ref[entry : entry + 1, :]).astype(F32)
    own = (row_of == seeds_ref[...]).astype(F32)
    spread_ref[:, :seeds] = counts.astype(BF16)
    spread_ref[:, seeds:] = own.astype(BF16)
    pick_ref[:seeds] = counts.T.astype(BF16)
    pick_ref[seeds:] = own.T.astype(BF16)


def activate(pre_ref, hidden_shape):
    pre_one = pre_ref[...].reshape(hidden_shape).astype(F32)
    sigmoid = jax.nn.sigmoid(pre_one)
    hidden = (pre_one * sigmoid).astype(BF16)
    return hidden, sigmoid * (1.0 + pre_one * (1.0 - sigmoid))


def mine_kernel(pre_ref, pick_ref, gathered_ref, slope_ref):
    half = slope_ref.shape[0]
    hidden, slope = activate(pre_ref, slope_ref.shape)
    gathered_ref[...] = contract(pick_ref[:, :half], hidden, 1, 0)
    slope_ref[...] = slope


def step_kernel(
    feat_ref,
    core_ref,
    pre_ref,
    gathered_ref,
    slope_ref,
    pick_ref,
    spread_ref,
    self_ref,
    neigh_ref,
    cotangent_ref,
    targets_ref,
    targets_other_ref,
    mine_ref,
    other_ref,
    output_ref,
    grads_ref,
    gathered,
    scratch,
):
    seeds = cotangent_ref.shape[0]
    columns = targets_ref.shape[0]
    half = slope_ref.shape[0]
    hidden, slope_other = activate(pre_ref.at[1 - core_ref[0]], slope_ref.shape)
    gathered[...] = contract(pick_ref[:, half:], hidden, 1, 0)
    picked = gathered_ref[...] + gathered[...]
    nbr_mean = (picked[:seeds] / FAN).astype(BF16)
    own = picked[seeds:].astype(BF16)
    pre_two = contract(own, self_ref[...], 1, 0) + contract(nbr_mean, neigh_ref[...], 1, 0)
    gate = jax.nn.sigmoid(pre_two)
    output_ref[...] = (pre_two * gate).astype(BF16)
    slope_two = (
        cotangent_ref[...].astype(F32) * (gate * (1.0 + pre_two * (1.0 - gate)))
    ).astype(BF16)

    scratch[0] = contract(own, slope_two, 0, 0)
    scratch[1] = contract(nbr_mean, slope_two, 0, 0)

    back = jnp.concatenate(
        [contract(slope_two, neigh_ref[...], 1, 1) / FAN, contract(slope_two, self_ref[...], 1, 1)],
        axis=0,
    )
    spread = spread_ref[...]
    back_hidden = contract(spread, back.astype(BF16), 1, 0)
    slope_one = jnp.concatenate(
        [
            (back_hidden[:half] * slope_ref[...]).astype(BF16),
            (back_hidden[half:] * slope_other).astype(BF16),
        ],
        axis=0,
    )
    inputs = jnp.concatenate(
        [
            jnp.concatenate([targets_ref[...], targets_other_ref[...]], axis=1),
            jnp.concatenate([mine_ref[...], other_ref[...]], axis=1),
        ],
        axis=0,
    )
    grad_one = contract(inputs, slope_one, 1, 0).astype(BF16)
    part_rows = (grads_ref.shape[1] - 2 * columns) // 2
    first = pl.multiple_of(feat_ref[0] * part_rows, part_rows)
    grad_two = jnp.concatenate(
        [scratch[0, pl.ds(first, part_rows), :], scratch[1, pl.ds(first, part_rows), :]], axis=0
    )
    every = jnp.concatenate([grad_one, grad_two.astype(BF16)], axis=0)
    for position in range(grads_ref.shape[0]):
        grads_ref[position] = every


def grads_kernel(parts_ref, output_ref, one_ref, two_ref, final_ref):
    final_ref[...] = output_ref[...]
    total = parts_ref[0].astype(F32)
    for position in range(1, parts_ref.shape[0]):
        total += parts_ref[position].astype(F32)
    columns, part_rows = one_ref.shape[1], two_ref.shape[1]
    one_ref[0] = total[:columns]
    one_ref[1] = total[columns : 2 * columns]
    two_ref[0] = total[2 * columns : 2 * columns + part_rows]
    two_ref[1] = total[2 * columns + part_rows :]


def run(kernel, outs, operands, scratch=(), limit=8, flops=0, specs=None):
    shapes = [jax.ShapeDtypeStruct(shape, dtype) for shape, dtype in outs]
    moved = sum(x.size * x.dtype.itemsize for x in operands) + sum(
        x.size * x.dtype.itemsize for x in shapes
    )
    if specs is None:
        specs = [SMEM if x.dtype == jnp.int32 and x.size == 1 else VMEM for x in operands]
    results = pl.pallas_call(
        kernel,
        out_shape=shapes,
        in_specs=specs,
        out_specs=[VMEM] * len(shapes),
        scratch_shapes=list(scratch),
        cost_estimate=pl.CostEstimate(flops=flops, bytes_accessed=moved, transcendentals=0),
        compiler_params=pltpu.CompilerParams(vmem_limit_bytes=limit * MIB),
    )(*operands)
    return results[0] if len(shapes) == 1 else results


def per_device(
    features,
    target_feats,
    tile_values,
    tile_index,
    tile_count,
    self_weight1,
    neigh_weight1,
    self_weight2,
    neigh_weight2,
    neighbors,
    seed_index,
    cotangent,
):
    src_rows, columns = features.shape
    tgt_rows = target_feats.shape[0]
    slots, block, _ = tile_values.shape
    hsize = self_weight2.shape[0]
    seeds = seed_index.shape[0]
    owners = lax.axis_size(NODE)
    near, far = lax.axis_size("zl"), lax.axis_size("zh")
    part_rows = hsize // lax.axis_size(FEAT)
    all_blocks = tgt_rows * owners // block
    half = tgt_rows // 2
    span = half // near
    core = lax.axis_index("c").reshape(1)
    feat = lax.axis_index(FEAT).reshape(1)
    halves = pltpu.VMEM((near, 2, columns, block), BF16)

    with jax.named_scope("aggregate_tiles"):
        aggregate = run(
            aggregate_kernel,
            [((all_blocks, columns, block), BF16)],
            (tile_count.reshape(1, 1), tile_index.T, tile_values, features.T),
            [
                pltpu.VMEM((src_rows // block, columns, block), BF16),
                pltpu.VMEM((slots, columns, block), F32),
                pltpu.VMEM((all_blocks, columns, block), F32),
            ],
            limit=56,
            specs=[VMEM, SMEM, VMEM, VMEM],
        )
    with jax.named_scope("aggregate_exchange"):
        parts = lax.all_to_all(
            aggregate.reshape(owners, tgt_rows // block * columns, block), NODE, 0, 0, tiled=True
        )
    with jax.named_scope("weights_gather"):
        weights = jnp.concatenate([self_weight1, neigh_weight1], axis=1)
        weights = lax.all_gather(weights, NEAR, tiled=True)
    with jax.named_scope("owned_sum"):
        blocks, targets_mine, targets_other, agg_mine, agg_other = run(
            owned_kernel,
            [((2 * near, 2 * columns, block), BF16)] + [((columns, half), BF16)] * 4,
            (core, parts, target_feats.T, weights),
            [halves],
            specs=[SMEM, VMEM, VMEM, ANY],
        )
    with jax.named_scope("near_exchange"):
        blocks = lax.all_to_all(blocks, NEAR, 0, 0, tiled=True)
    with jax.named_scope("partial_pre"):
        quarter = run(
            partial_kernel,
            [((span, hsize), BF16)],
            (blocks, weights),
            [pltpu.VMEM((4 * near * columns, span), BF16)],
        )
    with jax.named_scope("picks"):
        spread, pick = run(
            picks_kernel,
            [((tgt_rows, 2 * seeds), BF16), ((2 * seeds, tgt_rows), BF16)],
            (core, neighbors.T, seed_index.reshape(1, -1)),
            limit=16,
            flops=20 * tgt_rows * seeds,
        )
    with jax.named_scope("pre_sum_far"):
        parts = lax.all_gather(quarter, "zh")
        copies = run(
            far_kernel,
            [((near, span, hsize), BF16)],
            (parts, pick),
            specs=[VMEM, ANY],
        )
    with jax.named_scope("pre_gather"):
        pre_mine = lax.all_to_all(copies, "zl", 0, 0, tiled=True)
        pre_both = lax.all_gather(pre_mine, "c")
    with jax.named_scope("step_mine"):
        gathered, slope = run(
            mine_kernel,
            [((2 * seeds, hsize), F32), ((half, hsize), F32)],
            (pre_mine, pick),
            limit=12,
            flops=4 * seeds * half * hsize,
        )
    with jax.named_scope("step"):
        output, grads = run(
            step_kernel,
            [(cotangent.shape, BF16), ((owners, 2 * columns + 2 * part_rows, hsize), BF16)],
            (
                feat,
                core,
                pre_both,
                gathered,
                slope,
                pick,
                spread,
                self_weight2,
                neigh_weight2,
                cotangent,
                targets_mine,
                targets_other,
                agg_mine,
                agg_other,
            ),
            [
                pltpu.VMEM((2 * seeds, hsize), F32),
                pltpu.VMEM((2, hsize, hsize), F32),
            ],
            limit=24,
        )
    with jax.named_scope("grad_sum"):
        grads = lax.all_to_all(grads, NODE, 0, 0, tiled=True)
        grad_one, grad_two, output = run(
            grads_kernel,
            [((2, columns, hsize), F32), ((2, part_rows, hsize), F32), (cotangent.shape, BF16)],
            (grads, output),
        )
    return (output, grad_one, grad_two)


def solution(mesh):
    fine = Mesh(mesh.devices.reshape(4, 4, 2, 4, 4), FEAT + NODE)
    placed = (
        P(NODE, FEAT),
        P(NODE, FEAT),
        P(NODE, None, None),
        P(NODE, None),
        P(NODE),
        P(FEAT, None),
        P(FEAT, None),
        P(),
        P(),
        P(NODE, None),
        P(NODE),
        P(NODE, None),
    )
    return jax.shard_map(
        per_device,
        mesh=fine,
        in_specs=placed,
        out_specs=(P(NODE, None), P(None, FEAT, None), P(None, FEAT, None)),
        check_vma=False,
    )
```

```python
import jax
import jax.numpy as jnp
from jax import lax
from jax.experimental import pallas as pl
from jax.experimental.pallas import tpu as pltpu
from jax.sharding import Mesh
from jax.sharding import PartitionSpec as P

BF16 = jnp.bfloat16
F32 = jnp.float32
NODE = ("x", "y")
FEAT = ("zh", "zl", "c")
NEAR = ("zl", "c")
FAN = 10
MIB = 1 << 20

VMEM = pl.BlockSpec(memory_space=pltpu.VMEM)
ANY = pl.BlockSpec(memory_space=pl.ANY)
SMEM = pl.BlockSpec(memory_space=pltpu.SMEM)


def contract(left, right, left_dim, right_dim):
    return lax.dot_general(
        left, right, (((left_dim,), (right_dim,)), ((), ())), preferred_element_type=F32
    )


def aggregate_kernel(count_ref, index_ref, tiles_ref, feats_ref, out_ref, sources, products, total):
    slots, block, _ = tiles_ref.shape
    for position in range(sources.shape[0]):
        sources[position] = feats_ref[:, position * block : (position + 1) * block]
    out_ref[...] = jnp.zeros_like(out_ref)
    places = []
    for slot in range(slots):
        place = index_ref[0, slot]
        places.append(place)
        total[place] = jnp.zeros(total.shape[1:], F32)
    live_tiles = count_ref[...]
    for slot in range(slots):
        in_use = (slot < live_tiles).astype(F32)
        products[slot] = contract(sources[index_ref[1, slot]], tiles_ref[slot], 1, 1) * in_use
    for slot in range(slots):
        total[places[slot]] += products[slot]
    for slot in range(slots):
        out_ref[places[slot]] = total[places[slot]].astype(BF16)


def owned_kernel(parts_ref, targets_ref, weights_ref, blocks_ref):
    group, rows, block = blocks_ref.shape
    columns = rows // 2
    for position in range(group):
        blocks_ref[position, :columns] = targets_ref[:, position * block : (position + 1) * block]
        span = slice(position * columns, (position + 1) * columns)
        total = parts_ref[0, span].astype(F32)
        for source in range(1, parts_ref.shape[0]):
            total += parts_ref[source, span].astype(F32)
        blocks_ref[position, columns:] = total.astype(BF16)


def partial_kernel(blocks_ref, weights_ref, out_ref, inputs):
    group, rows, _ = blocks_ref.shape
    columns, hsize = rows // 2, out_ref.shape[1]
    depth = group * columns
    for position in range(group):
        first = position * columns
        inputs[first : first + columns] = blocks_ref[position, :columns]
        inputs[depth + first : depth + first + columns] = blocks_ref[position, columns:]
    total = contract(inputs[:depth], weights_ref[:, :hsize], 0, 0)
    total += contract(inputs[depth:], weights_ref[:, hsize:], 0, 0)
    out_ref[...] = total.astype(BF16)


def far_kernel(parts_ref, picks_ref, out_ref):
    total = parts_ref[0].astype(F32)
    for position in range(1, parts_ref.shape[0]):
        total += parts_ref[position].astype(F32)
    total = total.astype(BF16)
    for position in range(out_ref.shape[0]):
        out_ref[position] = total


def picks_kernel(core_ref, neighbors_ref, seeds_ref, spread_ref, pick_ref):
    fanout, seeds = neighbors_ref.shape
    rows = spread_ref.shape[0]
    step = lax.broadcasted_iota(jnp.int32, (rows, seeds), 0)
    half = rows // 2
    first = step // half
    lane = step % 128
    side = jnp.where(first == 0, core_ref[0], 1 - core_ref[0])
    row_of = ((step % half) // 128) * 256 + side * 128 + lane
    counts = jnp.zeros((rows, seeds), F32)
    for entry in range(fanout):
        counts += (row_of == neighbors_ref[entry : entry + 1, :]).astype(F32)
    own = (row_of == seeds_ref[...]).astype(F32)
    spread_ref[:, :seeds] = counts.astype(BF16)
    spread_ref[:, seeds:] = own.astype(BF16)
    pick_ref[:seeds] = counts.T.astype(BF16)
    pick_ref[seeds:] = own.T.astype(BF16)


def activate(pre_ref, hidden_shape):
    pre_one = pre_ref[...].reshape(hidden_shape).astype(F32)
    sigmoid = jax.nn.sigmoid(pre_one)
    hidden = (pre_one * sigmoid).astype(BF16)
    return hidden, sigmoid * (1.0 + pre_one * (1.0 - sigmoid))


def mine_kernel(core_ref, pre_ref, pick_ref, blocks_ref, gathered_ref, slope_ref, inputs_ref):
    group, _, block = blocks_ref.shape
    for position in range(group):
        side = core_ref[0] if 2 * position < group else 1 - core_ref[0]
        pair = position % (group // 2)
        inputs_ref[:, position * block : (position + 1) * block] = blocks_ref[2 * pair + side]
    half = slope_ref.shape[0]
    hidden, slope = activate(pre_ref, slope_ref.shape)
    gathered_ref[...] = contract(pick_ref[:, :half], hidden, 1, 0)
    slope_ref[...] = slope


def step_kernel(
    feat_ref,
    pre_ref,
    gathered_ref,
    slope_ref,
    pick_ref,
    spread_ref,
    self_ref,
    neigh_ref,
    cotangent_ref,
    inputs_ref,
    output_ref,
    grads_ref,
    gathered,
    scratch,
):
    seeds = cotangent_ref.shape[0]
    columns = inputs_ref.shape[0] // 2
    half = slope_ref.shape[0]
    hidden, slope_other = activate(pre_ref, slope_ref.shape)
    gathered[...] = contract(pick_ref[:, half:], hidden, 1, 0)
    picked = gathered_ref[...] + gathered[...]
    nbr_mean = (picked[:seeds] / FAN).astype(BF16)
    own = picked[seeds:].astype(BF16)
    pre_two = contract(own, self_ref[...], 1, 0) + contract(nbr_mean, neigh_ref[...], 1, 0)
    gate = jax.nn.sigmoid(pre_two)
    output_ref[...] = (pre_two * gate).astype(BF16)
    slope_two = (
        cotangent_ref[...].astype(F32) * (gate * (1.0 + pre_two * (1.0 - gate)))
    ).astype(BF16)

    scratch[0] = contract(own, slope_two, 0, 0)
    scratch[1] = contract(nbr_mean, slope_two, 0, 0)

    back = jnp.concatenate(
        [contract(slope_two, neigh_ref[...], 1, 1) / FAN, contract(slope_two, self_ref[...], 1, 1)],
        axis=0,
    )
    spread = spread_ref[...]
    back_hidden = contract(spread, back.astype(BF16), 1, 0)
    slope_one = jnp.concatenate(
        [
            (back_hidden[:half] * slope_ref[...]).astype(BF16),
            (back_hidden[half:] * slope_other).astype(BF16),
        ],
        axis=0,
    )
    grad_one = contract(inputs_ref[...], slope_one, 1, 0).astype(BF16)
    part_rows = (grads_ref.shape[1] - 2 * columns) // 2
    first = pl.multiple_of(feat_ref[0] * part_rows, part_rows)
    grad_two = jnp.concatenate(
        [scratch[0, pl.ds(first, part_rows), :], scratch[1, pl.ds(first, part_rows), :]], axis=0
    )
    every = jnp.concatenate([grad_one, grad_two.astype(BF16)], axis=0)
    for position in range(grads_ref.shape[0]):
        grads_ref[position] = every


def grads_kernel(parts_ref, output_ref, one_ref, two_ref, final_ref):
    final_ref[...] = output_ref[...]
    total = parts_ref[0].astype(F32)
    for position in range(1, parts_ref.shape[0]):
        total += parts_ref[position].astype(F32)
    columns, part_rows = one_ref.shape[1], two_ref.shape[1]
    one_ref[0] = total[:columns]
    one_ref[1] = total[columns : 2 * columns]
    two_ref[0] = total[2 * columns : 2 * columns + part_rows]
    two_ref[1] = total[2 * columns + part_rows :]


def run(kernel, outs, operands, scratch=(), limit=8, flops=0, specs=None):
    shapes = [jax.ShapeDtypeStruct(shape, dtype) for shape, dtype in outs]
    moved = sum(x.size * x.dtype.itemsize for x in operands) + sum(
        x.size * x.dtype.itemsize for x in shapes
    )
    if specs is None:
        specs = [SMEM if x.dtype == jnp.int32 and x.size == 1 else VMEM for x in operands]
    results = pl.pallas_call(
        kernel,
        out_shape=shapes,
        in_specs=specs,
        out_specs=[VMEM] * len(shapes),
        scratch_shapes=list(scratch),
        cost_estimate=pl.CostEstimate(flops=flops, bytes_accessed=moved, transcendentals=0),
        compiler_params=pltpu.CompilerParams(vmem_limit_bytes=limit * MIB),
    )(*operands)
    return results[0] if len(shapes) == 1 else results


def per_device(
    features,
    target_feats,
    tile_values,
    tile_index,
    tile_count,
    self_weight1,
    neigh_weight1,
    self_weight2,
    neigh_weight2,
    neighbors,
    seed_index,
    cotangent,
):
    src_rows, columns = features.shape
    tgt_rows = target_feats.shape[0]
    slots, block, _ = tile_values.shape
    hsize = self_weight2.shape[0]
    seeds = seed_index.shape[0]
    owners = lax.axis_size(NODE)
    near, far = lax.axis_size("zl"), lax.axis_size("zh")
    part_rows = hsize // lax.axis_size(FEAT)
    all_blocks = tgt_rows * owners // block
    half = tgt_rows // 2
    span = half // near
    core = lax.axis_index("c").reshape(1)
    feat = lax.axis_index(FEAT).reshape(1)
    swap = [(0, 1), (1, 0)]

    with jax.named_scope("aggregate_tiles"):
        aggregate = run(
            aggregate_kernel,
            [((all_blocks, columns, block), BF16)],
            (tile_count.reshape(1, 1), tile_index.T, tile_values, features.T),
            [
                pltpu.VMEM((src_rows // block, columns, block), BF16),
                pltpu.VMEM((slots, columns, block), F32),
                pltpu.VMEM((all_blocks, columns, block), F32),
            ],
            limit=56,
            specs=[VMEM, SMEM, VMEM, VMEM],
        )
    with jax.named_scope("aggregate_exchange"):
        parts = lax.all_to_all(
            aggregate.reshape(owners, tgt_rows // block * columns, block), NODE, 0, 0, tiled=True
        )
    with jax.named_scope("weights_gather"):
        weights = jnp.concatenate([self_weight1, neigh_weight1], axis=1)
        weights = lax.all_gather(weights, NEAR, tiled=True)
    with jax.named_scope("owned_sum"):
        owned = run(
            owned_kernel,
            [((2 * near, 2 * columns, block), BF16)],
            (parts, target_feats.T, weights),
            specs=[VMEM, VMEM, ANY],
        )
    with jax.named_scope("near_exchange"):
        blocks = lax.all_to_all(owned, NEAR, 0, 0, tiled=True)
    with jax.named_scope("partial_pre"):
        quarter = run(
            partial_kernel,
            [((span, hsize), BF16)],
            (blocks, weights),
            [pltpu.VMEM((4 * near * columns, span), BF16)],
        )
    with jax.named_scope("picks"):
        spread, pick = run(
            picks_kernel,
            [((tgt_rows, 2 * seeds), BF16), ((2 * seeds, tgt_rows), BF16)],
            (core, neighbors.T, seed_index.reshape(1, -1)),
            limit=16,
            flops=20 * tgt_rows * seeds,
        )
    with jax.named_scope("pre_sum_far"):
        parts = lax.all_gather(quarter, "zh")
        copies = run(
            far_kernel,
            [((near, span, hsize), BF16)],
            (parts, pick),
            specs=[VMEM, ANY],
        )
    with jax.named_scope("pre_gather"):
        pre_mine = lax.all_to_all(copies, "zl", 0, 0, tiled=True)
        pre_other = lax.ppermute(pre_mine, "c", swap)
    with jax.named_scope("step_mine"):
        gathered, slope, inputs = run(
            mine_kernel,
            [((2 * seeds, hsize), F32), ((half, hsize), F32), ((2 * columns, tgt_rows), BF16)],
            (core, pre_mine, pick, owned),
            limit=12,
            flops=4 * seeds * half * hsize,
        )
    with jax.named_scope("step"):
        output, grads = run(
            step_kernel,
            [(cotangent.shape, BF16), ((owners, 2 * columns + 2 * part_rows, hsize), BF16)],
            (
                feat,
                pre_other,
                gathered,
                slope,
                pick,
                spread,
                self_weight2,
                neigh_weight2,
                cotangent,
                inputs,
            ),
            [
                pltpu.VMEM((2 * seeds, hsize), F32),
                pltpu.VMEM((2, hsize, hsize), F32),
            ],
            limit=24,
        )
    with jax.named_scope("grad_sum"):
        grads = lax.all_to_all(grads, NODE, 0, 0, tiled=True)
        grad_one, grad_two, output = run(
            grads_kernel,
            [((2, columns, hsize), F32), ((2, part_rows, hsize), F32), (cotangent.shape, BF16)],
            (grads, output),
        )
    return (output, grad_one, grad_two)


def solution(mesh):
    fine = Mesh(mesh.devices.reshape(4, 4, 2, 4, 4), FEAT + NODE)
    placed = (
        P(NODE, FEAT),
        P(NODE, FEAT),
        P(NODE, None, None),
        P(NODE, None),
        P(NODE),
        P(FEAT, None),
        P(FEAT, None),
        P(),
        P(),
        P(NODE, None),
        P(NODE),
        P(NODE, None),
    )
    return jax.shard_map(
        per_device,
        mesh=fine,
        in_specs=placed,
        out_specs=(P(NODE, None), P(None, FEAT, None), P(None, FEAT, None)),
        check_vma=False,
    )
```
